256 devices in a mesh: scale: 4 (over z_lo, core), space: 64 (over x, z_hi, y).
Axes of the slice: x: 4, y: 4, z: 8 (z_hi: 4, z_lo: 2; z = z_hi * 2 + z_lo), core: 2. Of those that a mesh axis runs over, the one named last changes fastest.
Arguments:
- query_rows: bfloat16 [25088, 3584], P('space', 'scale'), may hold values from -8 to 8
- key_rows: bfloat16 [25088, 3584], P('space', 'scale'), may hold values from -8 to 8
- value_rows: bfloat16 [25088, 3584], P('space', 'scale'), may hold values from -24 to 24
- scale_index: int32 [512], replicated, may hold values from 0 to 5, as said below
- norm_gain: float32 [3584], P('scale'), may hold values from 0.1 to 1.9
- cotangent: bfloat16 [25088, 3584], P('space', 'scale'), may hold values from -6 to 6
Outputs:
- normed_out: bfloat16 [25088, 3584], P('space', 'scale')
- grad_query: bfloat16 [25088, 3584], P('space', 'scale')
- grad_key: bfloat16 [25088, 3584], P('space', 'scale')
- grad_value: bfloat16 [25088, 3584], P('space', 'scale')
The draws below stay inside these ranges and needn't reach their ends.
Inputs may be any that keep to these rules, and one draw needn't show every extreme that they name: `scale_index`: never falls along the coarse tokens; every level from 0 to 5 occurs.
All inputs are finite; a program needn't handle non-finite values.
Results may differ from the reference program's by a relative error of at most 0.033.
Values may be sent and summed in bfloat16 or wider, within the bound.
A program may use at most 128 MiB of HBM per device.

```python
import math
from functools import partial
import jax
import jax.numpy as jnp
from jax import lax

HEADS = 28
HEAD_DIM = 128
D = 3584
FT_DEV = 384
WIN = 192
CO_DEV = 8
LEVELS = 6
COARSE = 512
TOKENS = 25088
N_SPACE = 64


def draw_query_rows(key, part):
    key = jax.random.fold_in(key, 11)
    shape = (N_SPACE, FT_DEV + CO_DEV, D)
    sample = jnp.clip(jax.random.normal(key, shape, jnp.float32), -4.0, 4.0)
    return sample.reshape(TOKENS, D).astype(jnp.bfloat16)


def draw_key_rows(key, part):
    key = jax.random.fold_in(key, 12)
    shape = (N_SPACE, FT_DEV + CO_DEV, D)
    sample = jnp.clip(jax.random.normal(key, shape, jnp.float32), -4.0, 4.0)
    return sample.reshape(TOKENS, D).astype(jnp.bfloat16)


def draw_value_rows(key, part):
    key = jax.random.fold_in(key, 13)
    column_key, sample_key = jax.random.split(key)
    columns = jnp.arange(D, dtype=jnp.float32) / D
    jitter = jnp.exp(jax.random.uniform(column_key, (D,), jnp.float32, -0.3, 0.3))
    sample = jnp.clip(jax.random.normal(sample_key, (TOKENS, D), jnp.float32), -4.0, 4.0)
    column_scale = jnp.exp(math.log(3.0) * columns) * jitter
    return (sample * column_scale).astype(jnp.bfloat16)


def draw_scale_index(key, part):
    key = jax.random.fold_in(key, 5)
    shuffled = jax.random.permutation(key, COARSE - 1) + 1
    boundaries = jnp.sort(shuffled[:LEVELS - 1])
    positions = jnp.arange(COARSE)
    return jnp.sum((positions[:, None] >= boundaries[None, :]).astype(jnp.int32), axis=1).astype(jnp.int32)


def block_scale(key, extent, cuts, least, largest):
    loudness, own = 1.0, jax.random.fold_in(key, 6)
    for position, shards_of in cuts:
        steps = jnp.exp(jax.random.uniform(jax.random.fold_in(own, position), (shards_of,), jnp.float32, least / len(cuts), largest / len(cuts)))
        loudness = loudness * jnp.repeat(steps, extent[position] // shards_of).reshape([-1 if axis == position else 1 for axis in range(len(extent))])
    return loudness


def centred(stream_key, shape, width, most, cuts=(), kind=jnp.bfloat16):
    drawn = jax.random.normal(stream_key, shape, jnp.float32) * width
    if len(cuts) > 0:
        drawn = block_scale(stream_key, shape, cuts, -0.22, 0.18) * drawn
    return jnp.clip(drawn, min=-most, max=most).astype(kind)


def setup_inputs(seed: int = 0) -> dict:
    streams_of = jax.random.split(jax.random.key(seed), 7)
    query_rows = draw_query_rows(jax.random.fold_in(streams_of[6], 71), 0)
    key_rows = draw_key_rows(jax.random.fold_in(streams_of[6], 71), 0)
    value_rows = draw_value_rows(jax.random.fold_in(streams_of[6], 71), 0)
    scale_index = draw_scale_index(jax.random.fold_in(streams_of[6], 71), 0)
    norm_gain = jnp.clip(1.0 + 0.18 * jax.random.normal(streams_of[4], (D,), jnp.float32), 0.1, 1.9)
    cotangent = centred(streams_of[5], (TOKENS, D), 1.0, 6.0, ((0, 64), (1, 4)))
    return {"query_rows": query_rows, "key_rows": key_rows, "value_rows": value_rows, "scale_index": scale_index, "norm_gain": norm_gain, "cotangent": cotangent}


NEGATIVE = -1e+30

def rounded(tensor):
    return lax.optimization_barrier(tensor.astype(jnp.bfloat16)).astype(jnp.float32)

def neighbour_rows(tile_rows):
    padding = jnp.zeros((1,) + tile_rows.shape[1:], tile_rows.dtype)
    padded = jnp.concatenate([padding, tile_rows, padding], axis=0)
    return jnp.concatenate([padded[:-2], padded[1:-1], padded[2:]], axis=1)

def build_masks(scale_index):
    coarse_levels = scale_index.reshape(N_SPACE, CO_DEV)
    query_level = jnp.concatenate([jnp.full((N_SPACE, FT_DEV), LEVELS, jnp.int32), coarse_levels], axis=1)
    coarse_mask = scale_index[None, None, :] <= query_level[:, :, None]
    row_index = jnp.arange(FT_DEV + CO_DEV)[:, None]
    key_index = jnp.arange(3 * FT_DEV)[None, :] - FT_DEV
    nearby = (jnp.abs(row_index - key_index) <= WIN) & (row_index < FT_DEV)
    device = jnp.arange(N_SPACE)[:, None, None]
    owning = device + (key_index[None] + FT_DEV) // FT_DEV - 1
    inside = (owning >= 0) & (owning < N_SPACE)
    fine_mask = nearby[None] & inside
    return jnp.concatenate([coarse_mask, fine_mask], axis=2)

def head_keys(tile_rows):
    coarse = tile_rows[:, FT_DEV:].reshape(1, COARSE, HEAD_DIM)
    coarse = jnp.broadcast_to(coarse, (N_SPACE, COARSE, HEAD_DIM))
    return jnp.concatenate([coarse, neighbour_rows(tile_rows[:, :FT_DEV])], axis=1).astype(jnp.float32)

def head_forward(allowed, operands):
    query_head, key_head, value_head = operands
    key_heads = head_keys(key_head)
    values = head_keys(value_head)
    scores = jnp.einsum('nrd,nkd->nrk', query_head.astype(jnp.float32), key_heads) * HEAD_DIM ** (-0.5)
    row_peaks = lax.optimization_barrier(jnp.max(jnp.where(allowed, scores, NEGATIVE), axis=2, keepdims=True))
    weights = jnp.where(allowed, jnp.exp(scores - row_peaks), 0.0)
    totals = lax.optimization_barrier(jnp.sum(weights, axis=2, keepdims=True))
    summed = jnp.einsum('nrk,nkd->nrd', rounded(weights), values)
    attended = (summed / totals).astype(jnp.bfloat16)
    return (attended, (row_peaks + jnp.log(totals))[..., 0])

def fold_keys(partials):
    coarse = lax.optimization_barrier(jnp.sum(partials[:, :COARSE], axis=0)).reshape(N_SPACE, CO_DEV, HEAD_DIM)
    nearby = partials[:, COARSE:].reshape(N_SPACE, 3, FT_DEV, HEAD_DIM)
    blank_rows = jnp.zeros((1, FT_DEV, HEAD_DIM), jnp.float32)
    from_after = jnp.concatenate([nearby[1:, 0], blank_rows], axis=0)
    from_before = jnp.concatenate([blank_rows, nearby[:-1, 2]], axis=0)
    fine = nearby[:, 1] + from_after + from_before
    return jnp.concatenate([fine, coarse], axis=1).astype(jnp.bfloat16)

def head_backward(allowed, operands):
    query_head, key_head, value_head, grad_head, log_head, delta_head = operands
    key_heads = head_keys(key_head)
    values = head_keys(value_head)
    queries = query_head.astype(jnp.float32)
    grad_rows = grad_head.astype(jnp.float32)
    scaling = HEAD_DIM ** (-0.5)
    scores = jnp.einsum('nrd,nkd->nrk', queries, key_heads) * scaling
    row_probs = jnp.where(allowed, jnp.exp(scores - log_head[..., None]), 0.0)
    grad_values = jnp.einsum('nrk,nrd->nkd', rounded(row_probs), grad_rows)
    grad_probs = jnp.einsum('nrd,nkd->nrk', grad_rows, values)
    grad_scores = rounded(row_probs * (grad_probs - delta_head[..., None]))
    grad_queries = jnp.einsum('nrk,nkd->nrd', grad_scores, key_heads) * scaling
    grad_keys = jnp.einsum('nrk,nrd->nkd', grad_scores, queries) * scaling
    return (grad_queries.astype(jnp.bfloat16), fold_keys(grad_keys), fold_keys(grad_values))

def split_heads(tensor):
    return jnp.moveaxis(tensor.reshape(N_SPACE, FT_DEV + CO_DEV, HEADS, HEAD_DIM), 2, 0)

def join_heads(tensor):
    return jnp.moveaxis(tensor, 0, 2).reshape(N_SPACE * (FT_DEV + CO_DEV), HEADS * HEAD_DIM)

def reference(query_rows, key_rows, value_rows, scale_index, norm_gain, cotangent):
    allowed = build_masks(scale_index)
    heads_query = split_heads(query_rows)
    heads_key = split_heads(key_rows)
    heads_value = split_heads(value_rows)
    attended, log_totals = lax.map(partial(head_forward, allowed), (heads_query, heads_key, heads_value))
    attended_f = join_heads(attended).astype(jnp.float32)
    meansq = lax.optimization_barrier(jnp.mean(attended_f * attended_f, axis=1, keepdims=True)) + 1e-06
    inverse = lax.rsqrt(meansq)
    normed_out = (attended_f * inverse * norm_gain).astype(jnp.bfloat16)
    gained = norm_gain * cotangent.astype(jnp.float32)
    coupling = lax.optimization_barrier(jnp.mean(gained * attended_f, axis=1, keepdims=True))
    grad_attended = (inverse * gained - attended_f * inverse ** 3 * coupling).astype(jnp.bfloat16)
    products = grad_attended.astype(jnp.float32) * attended_f
    deltas = lax.optimization_barrier(jnp.sum(products.reshape(N_SPACE, FT_DEV + CO_DEV, HEADS, HEAD_DIM), axis=3))
    heads_delta = jnp.moveaxis(deltas, 2, 0)
    grad_query, grad_key, grad_value = lax.map(partial(head_backward, allowed), (heads_query, heads_key, heads_value, split_heads(grad_attended), log_totals, heads_delta))
    return (normed_out, join_heads(grad_query), join_heads(grad_key), join_heads(grad_value))
```

```python
import jax
import jax.numpy as jnp
from jax import lax
from jax.experimental import pallas as pl
from jax.experimental.pallas import tpu as pltpu
from jax.sharding import PartitionSpec as P

HEAD_DIM = 128
HEADS = 7
COLS = HEADS * HEAD_DIM
D = 3584
FINE = 384
WIN = 192
RIM = FINE + 2 * WIN
CO = 8
COARSE = 512
LEVELS = 6
SLOTS = 128
BLOCK = 128
SPAN = 512
NEG = -1e30
SCALING = HEAD_DIM ** (-0.5)
LOG2E = 1.4426950408889634
LN2 = 0.6931471805599453
F32 = jnp.float32
BF16 = jnp.bfloat16
MESH = pl.DeviceIdType.MESH

HALO = 0
AG_Y = 4
AG_Z = 7
AG_X = 10
AG_F = 18
STAT = 22
RS_OPP = 25
RS_X = 27
RS_Z = 31
RS_Y = 34
BACK = 37
COPIES = BACK + 2 * HEADS


def nt(a, b):
    return lax.dot_general(a, b, (((1,), (1,)), ((), ())), preferred_element_type=F32)


def nn(a, b):
    return lax.dot_general(a, b, (((1,), (0,)), ((), ())), preferred_element_type=F32)


def tn(a, b):
    return lax.dot_general(a, b, (((0,), (0,)), ((), ())), preferred_element_type=F32)


def head_cols(h):
    return pl.ds(pl.multiple_of(h * HEAD_DIM, HEAD_DIM), HEAD_DIM)


def diagonal(rows):
    slot = lax.broadcasted_iota(jnp.int32, (rows, COLS), 0) // CO
    column = lax.broadcasted_iota(jnp.int32, (rows, COLS), 1) // HEAD_DIM
    return slot == column


def spread(piece):
    return jnp.where(diagonal(SLOTS), jnp.concatenate([piece] * (SLOTS // CO), axis=0), 0.0)


def collect(wide):
    kept = jnp.where(diagonal(SLOTS), wide, 0.0)
    total = kept[0:CO]
    for g in range(1, HEADS):
        total = total + kept[g * CO : (g + 1) * CO]
    return total


def kernel(
    q, k, v, cot, kv16, qc, cotc, gain, lmask,
    of_n, of_q, of_k, of_v, oc,
    krim, vrim, cbuf, kc, vc, masks, gt, ot, dot, logs, deltas, dqt,
    stat, stat_in, qd, dod, gk, gv, dk, dv, own_k, own_v,
    opp_out, opp_in, x_out, x_in, z_out, z_in, y_out, y_in, back_out, back_in,
    send, recv,
):
    t = lax.axis_index("space")
    s = lax.axis_index("scale")
    x, z, y = t // 16, (t // 4) % 4, t % 4

    def at(xx, zz, yy):
        return {"space": xx * 16 + zz * 4 + yy}

    right = {"space": (t + 1) % 64}
    left = {"space": (t + 63) % 64}
    xr, xl = at((x + 1) % 4, z, y), at((x + 3) % 4, z, y)
    ys = [at(x, z, (y + d) % 4) for d in (1, 2, 3)]
    zs = [at(x, (z + d) % 4, y) for d in (1, 2, 3)]
    ss = [{"scale": (s + d) % 4} for d in (1, 2, 3)]

    def copy(src, dst, number, peer):
        return pltpu.make_async_remote_copy(
            src_ref=src, dst_ref=dst, send_sem=send.at[number], recv_sem=recv.at[number],
            device_id=peer, device_id_type=MESH,
        )

    pending = []

    def start(src, dst, number, peer):
        c = copy(src, dst, number, peer)
        c.start()
        pending.append(c)

    barrier = pltpu.get_barrier_semaphore()
    greeted = [left, right, xl, xr] + ys + zs + ss
    for peer in greeted:
        pl.semaphore_signal(barrier, inc=1, device_id=peer, device_id_type=MESH)
    pl.semaphore_wait(barrier, len(greeted))

    cbuf[t] = kv16[...]
    for d in (1, 2, 3):
        start(cbuf.at[t], cbuf.at[t], AG_Y + d - 1, ys[d - 1])
    halves = (
        (k, krim, slice(WIN, 2 * WIN), slice(0, WIN), right),
        (v, vrim, slice(WIN, 2 * WIN), slice(0, WIN), right),
        (k, krim, slice(0, WIN), slice(WIN + FINE, RIM), left),
        (v, vrim, slice(0, WIN), slice(WIN + FINE, RIM), left),
    )
    for n, (src, dst, a, b, peer) in enumerate(halves):
        start(src.at[a], dst.at[b], HALO + n, peer)

    def line(xx, zz):
        return cbuf.at[pl.ds(xx * 16 + zz * 4, 4)]

    for d in (1, 2, 3):
        got = cbuf.at[x * 16 + z * 4 + (y + 4 - d) % 4]
        copy(got, got, AG_Y + d - 1, ys[d - 1]).wait_recv()
    mine = line(x, z)
    for d in (1, 2, 3):
        start(mine, mine, AG_Z + d - 1, zs[d - 1])
    start(mine, mine, AG_X + 0, xr)
    start(mine, mine, AG_X + 4, xl)

    krim[WIN : WIN + FINE] = k[0:FINE]
    vrim[WIN : WIN + FINE] = v[0:FINE]
    row = lax.broadcasted_iota(jnp.int32, (SPAN, BLOCK), 0)
    column = lax.broadcasted_iota(jnp.int32, (SPAN, BLOCK), 1)
    for b in range(3):
        near = (row >= column) & (row - column <= 2 * WIN)
        place = row + b * BLOCK
        here = ((place >= WIN) | (t > 0)) & ((place < WIN + FINE) | (t < 63))
        masks[b] = jnp.where(near & here, 0.0, NEG)

    def prepare(h, _):
        cols = head_cols(h)
        gained = cot[0:FINE, cols].astype(F32) * gain[:, cols]
        for b in range(3):
            gt[h, :, b * BLOCK : (b + 1) * BLOCK] = gained[b * BLOCK : (b + 1) * BLOCK].T
        return 0

    for d in (1, 3, 2):
        block = line(x, (z + 4 - d) % 4)
        copy(block, block, AG_Z + d - 1, zs[d - 1]).wait_recv()
        start(block, block, AG_X + d, xr)
        start(block, block, AG_X + 4 + d, xl)

    lax.fori_loop(0, HEADS, prepare, 0)
    qd[...] = spread(qc[...]).astype(BF16)

    for d in (0, 1, 3, 2):
        zz = (z + 4 - d) % 4
        from_left, from_right = line((x + 3) % 4, zz), line((x + 1) % 4, zz)
        copy(from_left, from_left, AG_X + d, xr).wait_recv()
        if d in (0, 2):
            start(from_left, from_left, AG_F + d, xr)
        copy(from_right, from_right, AG_X + 4 + d, xl).wait_recv()
        if d in (1, 3):
            start(from_right, from_right, AG_F + d, xl)
    for n, (src, dst, a, b, peer) in enumerate(halves):
        copy(src.at[a], dst.at[b], HALO + n, peer).wait_recv()
    for d in (0, 1, 3, 2):
        far = line((x + 2) % 4, (z + 4 - d) % 4)
        copy(far, far, AG_F + d, xr if d in (0, 2) else xl).wait_recv()

    def forward(h, sums):
        cols = head_cols(h)
        both = cbuf[:, :, cols].astype(F32)
        keys = both[:, 0:CO].reshape(COARSE, HEAD_DIM).astype(BF16)
        values = both[:, CO:].reshape(COARSE, HEAD_DIM).astype(BF16)
        kc[:, cols] = keys
        vc[:, cols] = values
        out = []
        for b in range(3):
            rows = slice(b * BLOCK, (b + 1) * BLOCK)
            rim = slice(b * BLOCK, b * BLOCK + SPAN)
            queries = q[rows, cols]
            near = nt(krim[rim, cols], queries) * (SCALING * LOG2E) + masks[b]
            far = nt(keys, queries) * (SCALING * LOG2E)
            peak = jnp.maximum(
                jnp.max(near, axis=0, keepdims=True), jnp.max(far, axis=0, keepdims=True)
            )
            near, far = jnp.exp2(near - peak), jnp.exp2(far - peak)
            total = jnp.sum(near, axis=0, keepdims=True) + jnp.sum(far, axis=0, keepdims=True)
            summed = tn(vrim[rim, cols], near.astype(BF16)) + tn(values, far.astype(BF16))
            attended = (summed / total).astype(BF16)
            ot[h, :, rows] = attended
            logs[h, :, rows] = peak + jnp.log2(total)
            attended = attended.astype(F32)
            squares, crossed = sums[b]
            out.append((
                squares + jnp.sum(attended * attended, axis=0, keepdims=True),
                crossed + jnp.sum(attended * gt[h, :, rows], axis=0, keepdims=True),
            ))
        return tuple(out)

    nothing = jnp.zeros((1, BLOCK), F32)
    sums = lax.fori_loop(0, HEADS, forward, ((nothing, nothing),) * 3)

    scores = nt(qd[...], kc[...]) * (SCALING * LOG2E) + lmask[...]
    peak = jnp.max(scores, axis=1, keepdims=True)
    weights = jnp.exp2(scores - peak)
    total = jnp.sum(weights, axis=1, keepdims=True)
    wide = nn(weights.astype(BF16), vc[...]) / total
    log_c = peak + jnp.log2(total)
    attended_c = collect(wide).astype(BF16).astype(F32)
    gained_c = cotc[...] * gain[...]
    squares_c = jnp.sum(attended_c * attended_c, axis=1, keepdims=True)
    crossed_c = jnp.sum(attended_c * gained_c, axis=1, keepdims=True)

    stat[...] = jnp.zeros_like(stat)
    for b in range(3):
        stat[0:1, b * BLOCK : (b + 1) * BLOCK] = sums[b][0]
        stat[1:2, b * BLOCK : (b + 1) * BLOCK] = sums[b][1]
    stat[8:16, 0:BLOCK] = jnp.broadcast_to(squares_c, (CO, BLOCK))
    stat[8:16, BLOCK : 2 * BLOCK] = jnp.broadcast_to(crossed_c, (CO, BLOCK))
    for d in (1, 2, 3):
        start(stat, stat_in.at[d - 1], STAT + d - 1, ss[d - 1])
    for d in (1, 2, 3):
        copy(stat, stat_in.at[d - 1], STAT + d - 1, ss[d - 1]).wait_recv()
    whole = stat[...] + stat_in[0] + stat_in[1] + stat_in[2]
    inverse = lax.rsqrt(whole[0:1] / D + 1e-06)
    factor = inverse * inverse * inverse * (whole[1:2] / D)
    inverse_c = lax.rsqrt(whole[8:16, 0:1] / D + 1e-06)
    factor_c = inverse_c * inverse_c * inverse_c * (whole[8:16, BLOCK : BLOCK + 1] / D)

    oc[0] = attended_c * inverse_c * gain[...]
    grad_c = (inverse_c * gained_c - attended_c * factor_c).astype(BF16).astype(F32)
    grad_d = spread(grad_c)
    dod[...] = grad_d.astype(BF16)
    delta_c = jnp.sum(grad_d * spread(attended_c), axis=1, keepdims=True)

    def turn(h, _):
        attended = ot[h].astype(F32)
        grad = (inverse * gt[h] - attended * factor).astype(BF16)
        dot[h] = grad
        deltas[h] = jnp.sum(grad.astype(F32) * attended, axis=0, keepdims=True)
        return 0

    lax.fori_loop(0, HEADS, turn, 0)

    scores = nt(qd[...], kc[...]) * (SCALING * LOG2E) + lmask[...]
    probs = jnp.exp2(scores - log_c)
    grad_probs = nt(dod[...], vc[...])
    grad_scores = (probs * (grad_probs - delta_c)).astype(BF16)
    oc[1] = collect(nn(grad_scores, kc[...])) * SCALING
    gk[...] = tn(grad_scores, qd[...])
    gv[...] = tn(probs.astype(BF16), dod[...])

    def coarse_block(j, first):
        rows = pl.ds(pl.multiple_of(j * BLOCK, BLOCK), BLOCK)

        def body(h, _):
            cols = head_cols(h)
            keys, values = kc[rows, cols], vc[rows, cols]
            queries, grads = q[0:FINE, cols], dot[h]
            probs = jnp.exp2(nt(keys, queries) * (SCALING * LOG2E) - logs[h])
            grad_probs = nn(values, grads)
            grad_scores = (probs * (grad_probs - deltas[h])).astype(BF16)
            gv[rows, cols] = gv[rows, cols] + nt(probs.astype(BF16), grads)
            gk[rows, cols] = (gk[rows, cols] + nn(grad_scores, queries)) * SCALING
            part = tn(keys, grad_scores)
            dqt[h] = part if first else dqt[h] + part
            return 0

        lax.fori_loop(0, HEADS, body, 0)
        return rows

    rows = coarse_block((x + 2) % 4, True)
    opp_out[0] = gk[rows].astype(BF16)
    opp_out[1] = gv[rows].astype(BF16)
    start(opp_out.at[0], opp_in.at[0], RS_OPP, xr)
    start(opp_out.at[1], opp_in.at[1], RS_OPP + 1, xl)
    rows_r = coarse_block((x + 1) % 4, False)
    rows_l = coarse_block((x + 3) % 4, False)
    copy(opp_out.at[0], opp_in.at[0], RS_OPP, xr).wait_recv()
    x_out[0] = (gk[rows_r] + opp_in[0].astype(F32)).astype(BF16)
    x_out[1] = gv[rows_r].astype(BF16)
    start(x_out.at[0], x_in.at[0], RS_X, xr)
    start(x_out.at[1], x_in.at[1], RS_X + 1, xr)
    copy(opp_out.at[1], opp_in.at[1], RS_OPP + 1, xl).wait_recv()
    x_out[2] = gk[rows_l].astype(BF16)
    x_out[3] = (gv[rows_l] + opp_in[1].astype(F32)).astype(BF16)
    start(x_out.at[2], x_in.at[2], RS_X + 2, xl)
    start(x_out.at[3], x_in.at[3], RS_X + 3, xl)

    def fine(h, _):
        cols = head_cols(h)
        dk[...] = jnp.zeros_like(dk)
        dv[...] = jnp.zeros_like(dv)
        for b in range(3):
            rows = slice(b * BLOCK, (b + 1) * BLOCK)
            rim = slice(b * BLOCK, b * BLOCK + SPAN)
            keys, values = krim[rim, cols], vrim[rim, cols]
            queries, grads = q[rows, cols], dot[h, :, rows]
            scores = nt(keys, queries) * (SCALING * LOG2E) + masks[b]
            probs = jnp.exp2(scores - logs[h, :, rows])
            grad_probs = nn(values, grads)
            grad_scores = (probs * (grad_probs - deltas[h, :, rows])).astype(BF16)
            dv[rim] = dv[rim] + nt(probs.astype(BF16), grads)
            dk[rim] = dk[rim] + nn(grad_scores, queries)
            dqt[h, :, rows] = dqt[h, :, rows] + tn(keys, grad_scores)
        back_out[0, h, 0] = (dk[WIN + FINE : RIM] * SCALING).astype(BF16)
        back_out[0, h, 1] = dv[WIN + FINE : RIM].astype(BF16)
        back_out[1, h, 0] = (dk[0:WIN] * SCALING).astype(BF16)
        back_out[1, h, 1] = dv[0:WIN].astype(BF16)
        copy(back_out.at[0, h], back_in.at[0, h], BACK + h, right).start()
        copy(back_out.at[1, h], back_in.at[1, h], BACK + HEADS + h, left).start()
        own_k[h] = dk[WIN : WIN + FINE] * SCALING
        own_v[h] = dv[WIN : WIN + FINE]
        return 0

    lax.fori_loop(0, HEADS, fine, 0)
    own = coarse_block(x, False)

    for n in range(4):
        copy(x_out.at[n], x_in.at[n], RS_X + n, xr if n < 2 else xl).wait_recv()
    gk[own] = gk[own] + x_in[0].astype(F32) + x_in[2].astype(F32)
    gv[own] = gv[own] + x_in[1].astype(F32) + x_in[3].astype(F32)

    def piece(zz, yy, size):
        return pl.ds(pl.multiple_of(x * 128 + zz * 32 + yy * CO, size), size)

    for d in (1, 2, 3):
        there = piece((z + d) % 4, 0, 32)
        z_out[d - 1, 0] = gk[there].astype(BF16)
        z_out[d - 1, 1] = gv[there].astype(BF16)
        start(z_out.at[d - 1], z_in.at[d - 1], RS_Z + d - 1, zs[d - 1])

    def finish(h, _):
        cols = head_cols(h)
        for b in range(3):
            rows = slice(b * BLOCK, (b + 1) * BLOCK)
            of_q[rows, cols] = (dqt[h, :, rows] * SCALING).T.astype(BF16)
            normed = ot[h, :, rows].astype(F32) * inverse[:, rows]
            of_n[rows, cols] = (normed.T * gain[:, cols]).astype(BF16)
        return 0

    lax.fori_loop(0, HEADS, finish, 0)

    for d in (1, 2, 3):
        copy(z_out.at[d - 1], z_in.at[d - 1], RS_Z + d - 1, zs[d - 1]).wait_recv()
    here = piece(z, 0, 32)
    for n, total in enumerate((gk, gv)):
        total[here] = (
            total[here]
            + z_in[0, n].astype(F32) + z_in[1, n].astype(F32) + z_in[2, n].astype(F32)
        )
    for d in (1, 2, 3):
        there = piece(z, (y + d) % 4, CO)
        y_out[d - 1, 0] = gk[there]
        y_out[d - 1, 1] = gv[there]
        start(y_out.at[d - 1], y_in.at[d - 1], RS_Y + d - 1, ys[d - 1])

    def fold(h, _):
        cols = head_cols(h)
        copy(back_out.at[0, h], back_in.at[0, h], BACK + h, right).wait()
        copy(back_out.at[1, h], back_in.at[1, h], BACK + HEADS + h, left).wait()
        for side in range(2):
            rows = slice(side * WIN, (side + 1) * WIN)
            of_k[rows, cols] = (own_k[h, rows] + back_in[side, h, 0].astype(F32)).astype(BF16)
            of_v[rows, cols] = (own_v[h, rows] + back_in[side, h, 1].astype(F32)).astype(BF16)
        return 0

    lax.fori_loop(0, HEADS, fold, 0)

    for d in (1, 2, 3):
        copy(y_out.at[d - 1], y_in.at[d - 1], RS_Y + d - 1, ys[d - 1]).wait_recv()
    here = piece(z, y, CO)
    oc[2] = gk[here] + y_in[0, 0] + y_in[1, 0] + y_in[2, 0]
    oc[3] = gv[here] + y_in[0, 1] + y_in[1, 1] + y_in[2, 1]
    for c in pending:
        c.wait_send()


def on_device(query_rows, key_rows, value_rows, scale_index, norm_gain, cotangent):
    index_here = lax.axis_index("space")
    mine = lax.dynamic_slice_in_dim(scale_index, index_here * CO, CO)
    levels = jnp.concatenate([mine] * (SLOTS // CO))
    lmask = jnp.where(scale_index[None, :] <= levels[:, None], 0.0, NEG).astype(F32)
    kv16 = jnp.concatenate([key_rows[FINE:], value_rows[FINE:]])
    fine = jax.ShapeDtypeStruct((FINE, COLS), BF16)
    whole = pl.BlockSpec(memory_space=pltpu.VMEM)
    scratch = [
        pltpu.VMEM((RIM, COLS), BF16),
        pltpu.VMEM((RIM, COLS), BF16),
        pltpu.VMEM((64, 16, COLS), BF16),
        pltpu.VMEM((COARSE, COLS), BF16),
        pltpu.VMEM((COARSE, COLS), BF16),
        pltpu.VMEM((3, SPAN, BLOCK), F32),
        pltpu.VMEM((HEADS, HEAD_DIM, FINE), F32),
        pltpu.VMEM((HEADS, HEAD_DIM, FINE), BF16),
        pltpu.VMEM((HEADS, HEAD_DIM, FINE), BF16),
        pltpu.VMEM((HEADS, 1, FINE), F32),
        pltpu.VMEM((HEADS, 1, FINE), F32),
        pltpu.VMEM((HEADS, HEAD_DIM, FINE), F32),
        pltpu.VMEM((16, FINE), F32),
        pltpu.VMEM((3, 16, FINE), F32),
        pltpu.VMEM((SLOTS, COLS), BF16),
        pltpu.VMEM((SLOTS, COLS), BF16),
        pltpu.VMEM((COARSE, COLS), F32),
        pltpu.VMEM((COARSE, COLS), F32),
        pltpu.VMEM((RIM, HEAD_DIM), F32),
        pltpu.VMEM((RIM, HEAD_DIM), F32),
        pltpu.VMEM((HEADS, FINE, HEAD_DIM), F32),
        pltpu.VMEM((HEADS, FINE, HEAD_DIM), F32),
        pltpu.VMEM((2, BLOCK, COLS), BF16),
        pltpu.VMEM((2, BLOCK, COLS), BF16),
        pltpu.VMEM((4, BLOCK, COLS), BF16),
        pltpu.VMEM((4, BLOCK, COLS), BF16),
        pltpu.VMEM((3, 2, 32, COLS), BF16),
        pltpu.VMEM((3, 2, 32, COLS), BF16),
        pltpu.VMEM((3, 2, CO, COLS), F32),
        pltpu.VMEM((3, 2, CO, COLS), F32),
        pltpu.VMEM((2, HEADS, 2, WIN, HEAD_DIM), BF16),
        pltpu.VMEM((2, HEADS, 2, WIN, HEAD_DIM), BF16),
        pltpu.SemaphoreType.DMA((COPIES,)),
        pltpu.SemaphoreType.DMA((COPIES,)),
    ]
    outs = pl.pallas_call(
        kernel,
        out_shape=[fine] * 4 + [jax.ShapeDtypeStruct((4, CO, COLS), F32)],
        in_specs=[whole] * 9,
        out_specs=[whole] * 5,
        scratch_shapes=scratch,
        compiler_params=pltpu.CompilerParams(
            collective_id=0, has_side_effects=True, vmem_limit_bytes=56 * 1024 * 1024
        ),
    )(
        query_rows, key_rows, value_rows, cotangent, kv16,
        query_rows[FINE:].astype(F32), cotangent[FINE:].astype(F32), norm_gain[None, :], lmask,
    )
    return tuple(
        jnp.concatenate([outs[n], outs[4][n].astype(BF16)], axis=0) for n in range(4)
    )


def solution(mesh):
    both = P("space", "scale")
    return jax.shard_map(
        on_device, mesh=mesh, in_specs=(both, both, both, P(), P("scale"), both),
        out_specs=(both, both, both, both), check_vma=False,
    )
```

```python
import jax
import jax.numpy as jnp
from jax import lax
from jax.experimental import pallas as pl
from jax.experimental.pallas import tpu as pltpu
from jax.sharding import PartitionSpec as P

HEAD_DIM = 128
HEADS = 7
COLS = HEADS * HEAD_DIM
D = 3584
FINE = 384
WIN = 192
RIM = FINE + 2 * WIN
CO = 8
COARSE = 512
LEVELS = 6
SLOTS = 128
BLOCK = 128
SPAN = 512
NEG = -1e30
SCALING = HEAD_DIM ** (-0.5)
LOG2E = 1.4426950408889634
LN2 = 0.6931471805599453
F32 = jnp.float32
BF16 = jnp.bfloat16
MESH = pl.DeviceIdType.MESH

CHUNKS = 4
CHUNK = WIN // CHUNKS
HALO_K = 0
HALO_V = HALO_K + 2
HOP = HALO_V + 2 * CHUNKS
AG_Z = HOP + 2 * CHUNKS
AG_Y = AG_Z + 3
AG_X = AG_Y + 3
AG_F = AG_X + 8
STAT = AG_F + 4
RS_OPP = STAT + 3
RS_X = RS_OPP + 2
RS_Y = RS_X + 4
RS_Z = RS_Y + 3
BACK_K = RS_Z + 3
BACK_V = BACK_K + 2 * HEADS
BACK_HOP = BACK_V + 2 * HEADS
COPIES = BACK_HOP + 2 * HEADS


def nt(a, b):
    return lax.dot_general(a, b, (((1,), (1,)), ((), ())), preferred_element_type=F32)


def nn(a, b):
    return lax.dot_general(a, b, (((1,), (0,)), ((), ())), preferred_element_type=F32)


def tn(a, b):
    return lax.dot_general(a, b, (((0,), (0,)), ((), ())), preferred_element_type=F32)


def head_cols(h):
    return pl.ds(pl.multiple_of(h * HEAD_DIM, HEAD_DIM), HEAD_DIM)


def diagonal(rows):
    slot = lax.broadcasted_iota(jnp.int32, (rows, COLS), 0) // CO
    column = lax.broadcasted_iota(jnp.int32, (rows, COLS), 1) // HEAD_DIM
    return slot == column


def spread(piece):
    return jnp.where(diagonal(SLOTS), jnp.concatenate([piece] * (SLOTS // CO), axis=0), 0.0)


def collect(wide):
    kept = jnp.where(diagonal(SLOTS), wide, 0.0)
    total = kept[0:CO]
    for g in range(1, HEADS):
        total = total + kept[g * CO : (g + 1) * CO]
    return total


def kernel(
    q, k, v, cot, gain_ref, levels,
    of_n, of_q, of_k, of_v,
    krim, vrim, cbuf, kc, vc, masks, lmask, gt, ot, dot, logs, deltas, dqt,
    stat, stat_in, coarse_row, qd, dod, gk, gv, dk, dv, own_k, own_v,
    opp_out, opp_in, x_out, x_in, y_out, y_in, z_out, z_in, back_out, back_in,
    relay, back_relay, send, recv,
):
    t = lax.axis_index("space")
    s = lax.axis_index("scale")
    x, z, y = t // 16, (t // 4) % 4, t % 4

    def at(xx, zz, yy):
        return {"space": xx * 16 + zz * 4 + yy}

    right = {"space": (t + 1) % 64}
    left = {"space": (t + 63) % 64}
    xr, xl = at((x + 1) % 4, z, y), at((x + 3) % 4, z, y)
    ys = [at(x, z, (y + d) % 4) for d in (1, 2, 3)]
    zs = [at(x, (z + d) % 4, y) for d in (1, 2, 3)]
    ss = [{"scale": (s + d) % 4} for d in (1, 2, 3)]
    carry = [at((x + 1) % 4, (z + 1) % 4, y), at((x + 3) % 4, (z + 3) % 4, y)]

    edges = (y == 3, y == 0)
    relaying = (y == 0, y == 3)
    beside = (right, left)
    first_hop = (at(x, z, 0), at(x, z, 3))
    last_hop = (
        at((x + jnp.where(z == 3, 1, 0)) % 4, (z + 1) % 4, 0),
        at((x + jnp.where(z == 0, 3, 0)) % 4, (z + 3) % 4, 3),
    )

    def copy(src, dst, number, peer, out_number=None):
        return pltpu.make_async_remote_copy(
            src_ref=src, dst_ref=dst,
            send_sem=send.at[number if out_number is None else out_number],
            recv_sem=recv.at[number], device_id=peer, device_id_type=MESH,
        )

    pending = []

    def start(src, dst, number, peer):
        c = copy(src, dst, number, peer)
        c.start()
        pending.append(c)

    def depart(side, number, hop, src, via, dst):
        @pl.when(edges[side])
        def _():
            copy(src, via, hop, first_hop[side]).start()

        @pl.when(jnp.logical_not(edges[side]))
        def _():
            copy(src, dst, number, beside[side]).start()

    def pass_on(side, number, hop, via, dst):
        @pl.when(relaying[side])
        def _():
            copy(via, via, hop, first_hop[side]).wait_recv()
            copy(via, dst, number, last_hop[side], hop).start()

    def departed(side, number, hop, src):
        @pl.when(edges[side] | relaying[side])
        def _():
            copy(src, src, hop, beside[side]).wait_send()

        @pl.when(jnp.logical_not(edges[side]))
        def _():
            copy(src, src, number, beside[side]).wait_send()

    barrier = pltpu.get_barrier_semaphore()
    greeted = [left, right, xl, xr] + ys + zs + ss + carry
    for peer in greeted:
        pl.semaphore_signal(barrier, inc=1, device_id=peer, device_id_type=MESH)

    def tail(ref):
        return ref[...].astype(F32)[FINE:]

    gain = gain_ref[...].reshape(1, COLS)
    mine = x * 16 + y * 4 + z
    cbuf[mine] = jnp.concatenate([tail(k), tail(v)], axis=0).astype(BF16)
    pl.semaphore_wait(barrier, len(greeted))

    for d in (1, 2, 3):
        start(cbuf.at[mine], cbuf.at[mine], AG_Z + d - 1, zs[d - 1])

    def chunk(side, c):
        a = c * CHUNK + (WIN if side == 0 else 0)
        b = c * CHUNK + (0 if side == 0 else WIN + FINE)
        return (
            HALO_V + side * CHUNKS + c, HOP + side * CHUNKS + c,
            v.at[a : a + CHUNK], relay.at[c], vrim.at[b : b + CHUNK],
        )

    for c in range(CHUNKS):
        for side in range(2):
            depart(side, *chunk(side, c))
    halves = (
        (k, krim, slice(WIN, 2 * WIN), slice(0, WIN), right),
        (k, krim, slice(0, WIN), slice(WIN + FINE, RIM), left),
    )

    def pass_chunk(c):
        for side in range(2):
            number, hop, _, via, dst = chunk(side, c)
            pass_on(side, number, hop, via, dst)

    def line(xx, yy):
        return cbuf.at[pl.ds(xx * 16 + yy * 4, 4)]

    krim[WIN : WIN + FINE] = k[0:FINE]
    vrim[WIN : WIN + FINE] = v[0:FINE]
    for d in (1, 3, 2):
        got = cbuf.at[x * 16 + y * 4 + (z + 4 - d) % 4]
        copy(got, got, AG_Z + d - 1, zs[d - 1]).wait_recv()
    block = line(x, y)
    for d in (1, 3, 2):
        start(block, block, AG_Y + d - 1, ys[d - 1])
    start(block, block, AG_X + 0, xr)
    start(block, block, AG_X + 4, xl)
    for n, (src, dst, a, b, peer) in enumerate(halves):
        start(src.at[a], dst.at[b], HALO_K + n, peer)
    pass_chunk(0)

    row = lax.broadcasted_iota(jnp.int32, (SPAN, BLOCK), 0)
    column = lax.broadcasted_iota(jnp.int32, (SPAN, BLOCK), 1)
    for b in range(3):
        near = (row >= column) & (row - column <= 2 * WIN)
        place = row + b * BLOCK
        here = ((place >= WIN) | (t > 0)) & ((place < WIN + FINE) | (t < 63))
        masks[b] = jnp.where(near & here, 0.0, NEG)

    level = jnp.broadcast_to(levels[...].astype(F32).reshape(1, COARSE), (CO, COARSE))
    lane = lax.broadcasted_iota(jnp.int32, (CO, COARSE), 1)
    asked = lane == t * CO + lax.broadcasted_iota(jnp.int32, (CO, COARSE), 0)
    own_level = jnp.sum(jnp.where(asked, level, 0.0), axis=1, keepdims=True)
    seen = jnp.sum(jnp.where(level <= own_level, 1.0, 0.0), axis=1, keepdims=True)
    lane = lax.broadcasted_iota(jnp.int32, (SLOTS, COARSE), 1)
    order = (lane // 128) * 128 + ((lane // 8) % 4) * 32 + ((lane // 32) % 4) * 8 + lane % 8
    allowed = order.astype(F32) < jnp.concatenate([seen] * (SLOTS // CO), axis=0)
    lmask[...] = jnp.where(allowed, 0.0, NEG)
    pass_chunk(1)

    def prepare(h, _):
        cols = head_cols(h)
        gained = cot[0:FINE, cols].astype(F32) * gain_ref[cols].reshape(1, HEAD_DIM)
        for b in range(3):
            gt[h, :, b * BLOCK : (b + 1) * BLOCK] = gained[b * BLOCK : (b + 1) * BLOCK].T
        return 0

    lax.fori_loop(0, HEADS, prepare, 0)
    qd[...] = spread(tail(q)).astype(BF16)

    for d in (1, 3, 2):
        block = line(x, (y + 4 - d) % 4)
        copy(block, block, AG_Y + d - 1, ys[d - 1]).wait_recv()
        start(block, block, AG_X + d, xr)
        start(block, block, AG_X + 4 + d, xl)
    pass_chunk(2)

    for d in (0, 1, 3, 2):
        yy = (y + 4 - d) % 4
        from_left, from_right = line((x + 3) % 4, yy), line((x + 1) % 4, yy)
        copy(from_left, from_left, AG_X + d, xr).wait_recv()
        if d in (0, 2):
            start(from_left, from_left, AG_F + d, xr)
        copy(from_right, from_right, AG_X + 4 + d, xl).wait_recv()
        if d in (1, 3):
            start(from_right, from_right, AG_F + d, xl)
        if d == 1:
            pass_chunk(3)
    for n, (src, dst, a, b, peer) in enumerate(halves):
        copy(src.at[a], dst.at[b], HALO_K + n, peer).wait_recv()
    for c in range(CHUNKS):
        for side in range(2):
            number, _, _, _, dst = chunk(side, c)
            copy(dst, dst, number, beside[side]).wait_recv()
    for d in (0, 1, 3, 2):
        far = line((x + 2) % 4, (y + 4 - d) % 4)
        copy(far, far, AG_F + d, xr if d in (0, 2) else xl).wait_recv()

    def forward(h, sums):
        cols = head_cols(h)
        both = cbuf[:, :, cols].astype(F32)
        keys = both[:, 0:CO].reshape(COARSE, HEAD_DIM).astype(BF16)
        values = both[:, CO:].reshape(COARSE, HEAD_DIM).astype(BF16)
        kc[:, cols] = keys
        vc[:, cols] = values
        out = []
        for b in range(3):
            rows = slice(b * BLOCK, (b + 1) * BLOCK)
            rim = slice(b * BLOCK, b * BLOCK + SPAN)
            queries = q[rows, cols]
            near = nt(krim[rim, cols], queries) * (SCALING * LOG2E) + masks[b]
            far = nt(keys, queries) * (SCALING * LOG2E)
            peak = jnp.maximum(
                jnp.max(near, axis=0, keepdims=True), jnp.max(far, axis=0, keepdims=True)
            )
            near, far = jnp.exp2(near - peak), jnp.exp2(far - peak)
            total = jnp.sum(near, axis=0, keepdims=True) + jnp.sum(far, axis=0, keepdims=True)
            summed = tn(vrim[rim, cols], near.astype(BF16)) + tn(values, far.astype(BF16))
            attended = (summed / total).astype(BF16)
            ot[h, :, rows] = attended
            logs[h, :, rows] = peak + jnp.log2(total)
            attended = attended.astype(F32)
            squares, crossed = sums[b]
            out.append((
                squares + jnp.sum(attended * attended, axis=0, keepdims=True),
                crossed + jnp.sum(attended * gt[h, :, rows], axis=0, keepdims=True),
            ))
        return tuple(out)

    nothing = jnp.zeros((1, BLOCK), F32)
    sums = lax.fori_loop(0, HEADS, forward, ((nothing, nothing),) * 3)

    scores = nt(qd[...], kc[...]) * (SCALING * LOG2E) + lmask[...]
    peak = jnp.max(scores, axis=1, keepdims=True)
    weights = jnp.exp2(scores - peak)
    total = jnp.sum(weights, axis=1, keepdims=True)
    wide = nn(weights.astype(BF16), vc[...]) / total
    log_c = peak + jnp.log2(total)
    attended_c = collect(wide).astype(BF16).astype(F32)
    gained_c = tail(cot) * gain
    squares_c = jnp.sum(attended_c * attended_c, axis=1, keepdims=True)
    crossed_c = jnp.sum(attended_c * gained_c, axis=1, keepdims=True)

    stat[...] = jnp.zeros_like(stat)
    for b in range(3):
        stat[0:1, b * BLOCK : (b + 1) * BLOCK] = sums[b][0]
        stat[1:2, b * BLOCK : (b + 1) * BLOCK] = sums[b][1]
    stat[8:16, 0:BLOCK] = jnp.broadcast_to(squares_c, (CO, BLOCK))
    stat[8:16, BLOCK : 2 * BLOCK] = jnp.broadcast_to(crossed_c, (CO, BLOCK))
    for d in (1, 2, 3):
        start(stat, stat_in.at[d - 1], STAT + d - 1, ss[d - 1])
    for d in (1, 2, 3):
        copy(stat, stat_in.at[d - 1], STAT + d - 1, ss[d - 1]).wait_recv()
    whole = stat[...] + stat_in[0] + stat_in[1] + stat_in[2]
    inverse = lax.rsqrt(whole[0:1] / D + 1e-06)
    factor = inverse * inverse * inverse * (whole[1:2] / D)
    inverse_c = lax.rsqrt(whole[8:16, 0:1] / D + 1e-06)
    factor_c = inverse_c * inverse_c * inverse_c * (whole[8:16, BLOCK : BLOCK + 1] / D)

    normed_c = attended_c * inverse_c * gain
    grad_c = (inverse_c * gained_c - attended_c * factor_c).astype(BF16).astype(F32)
    grad_d = spread(grad_c)
    dod[...] = grad_d.astype(BF16)
    delta_c = jnp.sum(grad_d * spread(attended_c), axis=1, keepdims=True)

    def turn(h, _):
        attended = ot[h].astype(F32)
        grad = (inverse * gt[h] - attended * factor).astype(BF16)
        dot[h] = grad
        deltas[h] = jnp.sum(grad.astype(F32) * attended, axis=0, keepdims=True)
        return 0

    lax.fori_loop(0, HEADS, turn, 0)

    scores = nt(qd[...], kc[...]) * (SCALING * LOG2E) + lmask[...]
    probs = jnp.exp2(scores - log_c)
    grad_probs = nt(dod[...], vc[...])
    grad_scores = (probs * (grad_probs - delta_c)).astype(BF16)
    query_c = collect(nn(grad_scores, kc[...])) * SCALING
    coarse_row[0] = normed_c
    coarse_row[1] = query_c
    gk[...] = tn(grad_scores, qd[...])
    gv[...] = tn(probs.astype(BF16), dod[...])

    def coarse_block(j, first):
        rows = pl.ds(pl.multiple_of(j * BLOCK, BLOCK), BLOCK)

        def body(h, _):
            cols = head_cols(h)
            keys, values = kc[rows, cols], vc[rows, cols]
            queries, grads = q[0:FINE, cols], dot[h]
            probs = jnp.exp2(nt(keys, queries) * (SCALING * LOG2E) - logs[h])
            grad_probs = nn(values, grads)
            grad_scores = (probs * (grad_probs - deltas[h])).astype(BF16)
            gv[rows, cols] = gv[rows, cols] + nt(probs.astype(BF16), grads)
            gk[rows, cols] = (gk[rows, cols] + nn(grad_scores, queries)) * SCALING
            part = tn(keys, grad_scores)
            dqt[h] = part if first else dqt[h] + part
            return 0

        lax.fori_loop(0, HEADS, body, 0)
        return rows

    rows = coarse_block((x + 2) % 4, True)
    opp_out[0] = gk[rows].astype(BF16)
    opp_out[1] = gv[rows].astype(BF16)
    start(opp_out.at[0], opp_in.at[0], RS_OPP, xr)
    start(opp_out.at[1], opp_in.at[1], RS_OPP + 1, xl)
    rows_r = coarse_block((x + 1) % 4, False)
    rows_l = coarse_block((x + 3) % 4, False)
    copy(opp_out.at[0], opp_in.at[0], RS_OPP, xr).wait_recv()
    x_out[0] = (gk[rows_r] + opp_in[0].astype(F32)).astype(BF16)
    x_out[1] = gv[rows_r].astype(BF16)
    start(x_out.at[0], x_in.at[0], RS_X, xr)
    start(x_out.at[1], x_in.at[1], RS_X + 1, xr)
    copy(opp_out.at[1], opp_in.at[1], RS_OPP + 1, xl).wait_recv()
    x_out[2] = gk[rows_l].astype(BF16)
    x_out[3] = (gv[rows_l] + opp_in[1].astype(F32)).astype(BF16)
    start(x_out.at[2], x_in.at[2], RS_X + 2, xl)
    start(x_out.at[3], x_in.at[3], RS_X + 3, xl)

    def fine(h, _):
        cols = head_cols(h)
        dk[...] = jnp.zeros_like(dk)
        dv[...] = jnp.zeros_like(dv)
        for b in range(3):
            rows = slice(b * BLOCK, (b + 1) * BLOCK)
            rim = slice(b * BLOCK, b * BLOCK + SPAN)
            keys, values = krim[rim, cols], vrim[rim, cols]
            queries, grads = q[rows, cols], dot[h, :, rows]
            scores = nt(keys, queries) * (SCALING * LOG2E) + masks[b]
            probs = jnp.exp2(scores - logs[h, :, rows])
            grad_probs = nn(values, grads)
            grad_scores = (probs * (grad_probs - deltas[h, :, rows])).astype(BF16)
            dv[rim] = dv[rim] + nt(probs.astype(BF16), grads)
            dk[rim] = dk[rim] + nn(grad_scores, queries)
            dqt[h, :, rows] = dqt[h, :, rows] + tn(keys, grad_scores)
        for side in range(2):
            part = slice(WIN + FINE, RIM) if side == 0 else slice(0, WIN)
            back_out[side, h, 0] = (dk[part] * SCALING).astype(BF16)
            back_out[side, h, 1] = dv[part].astype(BF16)
            depart(side, *back(side, h))
            copy(
                back_out.at[side, h, 0], back_in.at[side, h, 0], BACK_K + side * HEADS + h,
                beside[side],
            ).start()
        own_k[h] = dk[WIN : WIN + FINE] * SCALING
        own_v[h] = dv[WIN : WIN + FINE]
        return 0

    def back(side, h):
        return (
            BACK_V + side * HEADS + h, BACK_HOP + side * HEADS + h,
            back_out.at[side, h, 1], back_relay.at[h], back_in.at[side, h, 1],
        )

    def pass_back(first, last):
        def body(h, _):
            for side in range(2):
                number, hop, _, via, dst = back(side, h)
                pass_on(side, number, hop, via, dst)
            return 0

        lax.fori_loop(first, last, body, 0)

    lax.fori_loop(0, HEADS, fine, 0)
    own = coarse_block(x, False)
    pass_back(0, 3)

    for n in range(4):
        copy(x_out.at[n], x_in.at[n], RS_X + n, xr if n < 2 else xl).wait_recv()
    gk[own] = gk[own] + x_in[0].astype(F32) + x_in[2].astype(F32)
    gv[own] = gv[own] + x_in[1].astype(F32) + x_in[3].astype(F32)

    def piece(yy, zz, size):
        return pl.ds(pl.multiple_of(x * 128 + yy * 32 + zz * CO, size), size)

    for d in (1, 2, 3):
        there = piece((y + d) % 4, 0, 32)
        y_out[d - 1, 0] = gk[there].astype(BF16)
        y_out[d - 1, 1] = gv[there].astype(BF16)
        start(y_out.at[d - 1], y_in.at[d - 1], RS_Y + d - 1, ys[d - 1])
    pass_back(3, 5)

    def finish(h, _):
        cols = head_cols(h)
        own_gain = gain_ref[cols].reshape(1, HEAD_DIM)
        queries, normed = [], []
        for b in range(3):
            rows = slice(b * BLOCK, (b + 1) * BLOCK)
            queries.append((dqt[h, :, rows] * SCALING).T)
            normed.append((ot[h, :, rows].astype(F32) * inverse[:, rows]).T * own_gain)
        of_n[:, cols] = jnp.concatenate(normed + [coarse_row[0, :, cols]], axis=0).astype(BF16)
        of_q[:, cols] = jnp.concatenate(queries + [coarse_row[1, :, cols]], axis=0).astype(BF16)
        return 0

    lax.fori_loop(0, HEADS, finish, 0)
    pass_back(5, 7)

    for d in (1, 2, 3):
        copy(y_out.at[d - 1], y_in.at[d - 1], RS_Y + d - 1, ys[d - 1]).wait_recv()
    here = piece(y, 0, 32)
    for n, total in enumerate((gk, gv)):
        total[here] = (
            total[here]
            + y_in[0, n].astype(F32) + y_in[1, n].astype(F32) + y_in[2, n].astype(F32)
        )
    for d in (1, 2, 3):
        there = piece(y, (z + d) % 4, CO)
        z_out[d - 1, 0] = gk[there]
        z_out[d - 1, 1] = gv[there]
        start(z_out.at[d - 1], z_in.at[d - 1], RS_Z + d - 1, zs[d - 1])
    for d in (1, 2, 3):
        copy(z_out.at[d - 1], z_in.at[d - 1], RS_Z + d - 1, zs[d - 1]).wait_recv()
    here = piece(y, z, CO)
    coarse_row[0] = gk[here] + z_in[0, 0] + z_in[1, 0] + z_in[2, 0]
    coarse_row[1] = gv[here] + z_in[0, 1] + z_in[1, 1] + z_in[2, 1]

    def fold(h, _):
        cols = head_cols(h)
        for side in range(2):
            number, hop, src, _, dst = back(side, h)
            copy(dst, dst, number, beside[side]).wait_recv()
            departed(side, number, hop, src)
            copy(
                back_out.at[side, h, 0], back_in.at[side, h, 0], BACK_K + side * HEADS + h,
                beside[side],
            ).wait()
        for n, (mine, target) in enumerate(((own_k, of_k), (own_v, of_v))):
            parts = [
                mine[h, side * WIN : (side + 1) * WIN] + back_in[side, h, n].astype(F32)
                for side in range(2)
            ]
            target[:, cols] = jnp.concatenate(
                parts + [coarse_row[n, :, cols]], axis=0
            ).astype(BF16)
        return 0

    lax.fori_loop(0, HEADS, fold, 0)
    for c in range(CHUNKS):
        for side in range(2):
            number, hop, src, _, _ = chunk(side, c)
            departed(side, number, hop, src)
    for c in pending:
        c.wait_send()


def on_device(query_rows, key_rows, value_rows, scale_index, norm_gain, cotangent):
    full = jax.ShapeDtypeStruct((FINE + CO, COLS), BF16)
    whole = pl.BlockSpec(memory_space=pltpu.VMEM)
    scratch = [
        pltpu.VMEM((RIM, COLS), BF16),
        pltpu.VMEM((RIM, COLS), BF16),
        pltpu.VMEM((64, 16, COLS), BF16),
        pltpu.VMEM((COARSE, COLS), BF16),
        pltpu.VMEM((COARSE, COLS), BF16),
        pltpu.VMEM((3, SPAN, BLOCK), F32),
        pltpu.VMEM((SLOTS, COARSE), F32),
        pltpu.VMEM((HEADS, HEAD_DIM, FINE), F32),
        pltpu.VMEM((HEADS, HEAD_DIM, FINE), BF16),
        pltpu.VMEM((HEADS, HEAD_DIM, FINE), BF16),
        pltpu.VMEM((HEADS, 1, FINE), F32),
        pltpu.VMEM((HEADS, 1, FINE), F32),
        pltpu.VMEM((HEADS, HEAD_DIM, FINE), F32),
        pltpu.VMEM((16, FINE), F32),
        pltpu.VMEM((3, 16, FINE), F32),
        pltpu.VMEM((2, CO, COLS), F32),
        pltpu.VMEM((SLOTS, COLS), BF16),
        pltpu.VMEM((SLOTS, COLS), BF16),
        pltpu.VMEM((COARSE, COLS), F32),
        pltpu.VMEM((COARSE, COLS), F32),
        pltpu.VMEM((RIM, HEAD_DIM), F32),
        pltpu.VMEM((RIM, HEAD_DIM), F32),
        pltpu.VMEM((HEADS, FINE, HEAD_DIM), F32),
        pltpu.VMEM((HEADS, FINE, HEAD_DIM), F32),
        pltpu.VMEM((2, BLOCK, COLS), BF16),
        pltpu.VMEM((2, BLOCK, COLS), BF16),
        pltpu.VMEM((4, BLOCK, COLS), BF16),
        pltpu.VMEM((4, BLOCK, COLS), BF16),
        pltpu.VMEM((3, 2, 32, COLS), BF16),
        pltpu.VMEM((3, 2, 32, COLS), BF16),
        pltpu.VMEM((3, 2, CO, COLS), F32),
        pltpu.VMEM((3, 2, CO, COLS), F32),
        pltpu.VMEM((2, HEADS, 2, WIN, HEAD_DIM), BF16),
        pltpu.VMEM((2, HEADS, 2, WIN, HEAD_DIM), BF16),
        pltpu.VMEM((CHUNKS, CHUNK, COLS), BF16),
        pltpu.VMEM((HEADS, WIN, HEAD_DIM), BF16),
        pltpu.SemaphoreType.DMA((COPIES,)),
        pltpu.SemaphoreType.DMA((COPIES,)),
    ]
    return tuple(pl.pallas_call(
        kernel,
        out_shape=[full] * 4,
        in_specs=[whole] * 6,
        out_specs=[whole] * 4,
        scratch_shapes=scratch,
        compiler_params=pltpu.CompilerParams(
            collective_id=0, has_side_effects=True, vmem_limit_bytes=56 * 1024 * 1024
        ),
    )(query_rows, key_rows, value_rows, cotangent, norm_gain, scale_index))


def solution(mesh):
    both = P("space", "scale")
    return jax.shard_map(
        on_device, mesh=mesh, in_specs=(both, both, both, P(), P("scale"), both),
        out_specs=(both, both, both, both), check_vma=False,
    )
```

```python
import jax
import jax.numpy as jnp
from jax import lax
from jax.experimental import pallas as pl
from jax.experimental.pallas import tpu as pltpu
from jax.sharding import PartitionSpec as P

HEAD_DIM = 128
HEADS = 7
COLS = HEADS * HEAD_DIM
D = 3584
FINE = 384
WIN = 192
RIM = FINE + 2 * WIN
CO = 8
COARSE = 512
LEVELS = 6
SLOTS = 128
BLOCK = 128
SPAN = 512
OWN = ((192, 512), (192, 576), (256, 576))
HALO = (((0, 192),), ((128, 192), (576, 640)), ((576, 768),))
NEG = -1e30
SCALING = HEAD_DIM ** (-0.5)
LOG2E = 1.4426950408889634
LN2 = 0.6931471805599453
F32 = jnp.float32
BF16 = jnp.bfloat16
MESH = pl.DeviceIdType.MESH

CHUNKS = 4
CHUNK = WIN // CHUNKS
HALO_K = 0
HALO_V = HALO_K + 2
HOP = HALO_V + 2 * CHUNKS
AG_Z = HOP + 2 * CHUNKS
AG_Y = AG_Z + 3
AG_X = AG_Y + 3
AG_F = AG_X + 8
STAT = AG_F + 4
RS_OPP = STAT + 3
RS_X = RS_OPP + 2
RS_Y = RS_X + 4
RS_Z = RS_Y + 3
BACK_K = RS_Z + 3
BACK_V = BACK_K + 2 * HEADS
BACK_HOP = BACK_V + 2 * HEADS
COPIES = BACK_HOP + 2 * HEADS


def nt(a, b):
    return lax.dot_general(a, b, (((1,), (1,)), ((), ())), preferred_element_type=F32)


def nn(a, b):
    return lax.dot_general(a, b, (((1,), (0,)), ((), ())), preferred_element_type=F32)


def tn(a, b):
    return lax.dot_general(a, b, (((0,), (0,)), ((), ())), preferred_element_type=F32)


def every_head(body, carry=0, first=0, last=HEADS):
    for h in range(first, last):
        carry = body(h, carry)
    return carry


def head_cols(h):
    if isinstance(h, int):
        return slice(h * HEAD_DIM, (h + 1) * HEAD_DIM)
    return pl.ds(pl.multiple_of(h * HEAD_DIM, HEAD_DIM), HEAD_DIM)


def diagonal(rows):
    slot = lax.broadcasted_iota(jnp.int32, (rows, COLS), 0) // CO
    column = lax.broadcasted_iota(jnp.int32, (rows, COLS), 1) // HEAD_DIM
    return slot == column


def spread(piece):
    return jnp.where(diagonal(SLOTS), jnp.concatenate([piece] * (SLOTS // CO), axis=0), 0.0)


def collect(wide):
    kept = jnp.where(diagonal(SLOTS), wide, 0.0)
    total = kept[0:CO]
    for g in range(1, HEADS):
        total = total + kept[g * CO : (g + 1) * CO]
    return total


def kernel(
    q, k, v, cot, gain_ref, levels,
    of_n, of_q, of_k, of_v,
    krim, vrim, cbuf, kc, vc, masks, lmask, gt, ot, dot, logs, deltas, dqt,
    stat, stat_in, coarse_row, qd, dod, gk, gv, peaks, totals, summed, own_k, own_v,
    opp_out, opp_in, x_out, x_in, y_out, y_in, z_out, z_in, back_out, back_in,
    relay, back_relay, send, recv,
):
    t = lax.axis_index("space")
    s = lax.axis_index("scale")
    x, z, y = t // 16, (t // 4) % 4, t % 4

    def at(xx, zz, yy):
        return {"space": xx * 16 + zz * 4 + yy}

    right = {"space": (t + 1) % 64}
    left = {"space": (t + 63) % 64}
    xr, xl = at((x + 1) % 4, z, y), at((x + 3) % 4, z, y)
    ys = [at(x, z, (y + d) % 4) for d in (1, 2, 3)]
    zs = [at(x, (z + d) % 4, y) for d in (1, 2, 3)]
    ss = [{"scale": (s + d) % 4} for d in (1, 2, 3)]
    carry = [at((x + 1) % 4, (z + 1) % 4, y), at((x + 3) % 4, (z + 3) % 4, y)]

    edges = (y == 3, y == 0)
    relaying = (y == 0, y == 3)
    beside = (right, left)
    first_hop = (at(x, z, 0), at(x, z, 3))
    last_hop = (
        at((x + jnp.where(z == 3, 1, 0)) % 4, (z + 1) % 4, 0),
        at((x + jnp.where(z == 0, 3, 0)) % 4, (z + 3) % 4, 3),
    )

    def copy(src, dst, number, peer, out_number=None):
        return pltpu.make_async_remote_copy(
            src_ref=src, dst_ref=dst,
            send_sem=send.at[number if out_number is None else out_number],
            recv_sem=recv.at[number], device_id=peer, device_id_type=MESH,
        )

    pending = []

    def start(src, dst, number, peer):
        c = copy(src, dst, number, peer)
        c.start()
        pending.append(c)

    def depart(side, number, hop, src, via, dst):
        @pl.when(edges[side])
        def _():
            copy(src, via, hop, first_hop[side]).start()

        @pl.when(jnp.logical_not(edges[side]))
        def _():
            copy(src, dst, number, beside[side]).start()

    def pass_on(side, number, hop, via, dst):
        @pl.when(relaying[side])
        def _():
            copy(via, via, hop, first_hop[side]).wait_recv()
            copy(via, dst, number, last_hop[side], hop).start()

    def departed(side, number, hop, src):
        @pl.when(edges[side] | relaying[side])
        def _():
            copy(src, src, hop, beside[side]).wait_send()

        @pl.when(jnp.logical_not(edges[side]))
        def _():
            copy(src, src, number, beside[side]).wait_send()

    barrier = pltpu.get_barrier_semaphore()
    greeted = [left, right, xl, xr] + ys + zs + ss + carry
    for peer in greeted:
        pl.semaphore_signal(barrier, inc=1, device_id=peer, device_id_type=MESH)

    def tail(ref):
        return ref[...].astype(F32)[FINE:]

    gain = gain_ref[...].reshape(1, COLS)
    mine = x * 16 + y * 4 + z
    cbuf[mine] = jnp.concatenate([tail(k), tail(v)], axis=0).astype(BF16)
    pl.semaphore_wait(barrier, len(greeted))

    for d in (1, 2, 3):
        start(cbuf.at[mine], cbuf.at[mine], AG_Z + d - 1, zs[d - 1])

    def chunk(side, c):
        a = c * CHUNK + (WIN if side == 0 else 0)
        b = c * CHUNK + (0 if side == 0 else WIN + FINE)
        return (
            HALO_V + side * CHUNKS + c, HOP + side * CHUNKS + c,
            v.at[a : a + CHUNK], relay.at[c], vrim.at[b : b + CHUNK],
        )

    for c in range(CHUNKS):
        for side in range(2):
            depart(side, *chunk(side, c))
    halves = (
        (k, krim, slice(WIN, 2 * WIN), slice(0, WIN), right),
        (k, krim, slice(0, WIN), slice(WIN + FINE, RIM), left),
    )

    def pass_chunk(c):
        for side in range(2):
            number, hop, _, via, dst = chunk(side, c)
            pass_on(side, number, hop, via, dst)

    def line(xx, yy):
        return cbuf.at[pl.ds(xx * 16 + yy * 4, 4)]

    krim[WIN : WIN + FINE] = k[0:FINE]
    vrim[WIN : WIN + FINE] = v[0:FINE]
    row = lax.broadcasted_iota(jnp.int32, (SPAN, BLOCK), 0)
    column = lax.broadcasted_iota(jnp.int32, (SPAN, BLOCK), 1)
    for b in range(3):
        near = (row >= column) & (row - column <= 2 * WIN)
        place = row + b * BLOCK
        here = ((place >= WIN) | (t > 0)) & ((place < WIN + FINE) | (t < 63))
        masks[b] = jnp.where(near & here, 0.0, NEG)

    nothing = jnp.zeros((1, BLOCK), F32)

    def masked(b, first, last):
        return masks[b, first - b * BLOCK : last - b * BLOCK]

    def own_keys(h, _):
        cols = head_cols(h)
        for b in range(3):
            rows = slice(b * BLOCK, (b + 1) * BLOCK)
            first, last = OWN[b]
            scores = nt(krim[first:last, cols], q[rows, cols]) * (SCALING * LOG2E)
            scores = scores + masked(b, first, last)
            peak = jnp.max(scores, axis=0, keepdims=True)
            weights = jnp.exp2(scores - peak)
            peaks[h, :, rows] = peak
            totals[h, :, rows] = jnp.sum(weights, axis=0, keepdims=True)
            summed[h, :, rows] = tn(vrim[first:last, cols], weights.astype(BF16))
        return 0

    every_head(own_keys, 0, 0, 2)
    for d in (1, 3, 2):
        got = cbuf.at[x * 16 + y * 4 + (z + 4 - d) % 4]
        copy(got, got, AG_Z + d - 1, zs[d - 1]).wait_recv()
    block = line(x, y)
    for d in (1, 3, 2):
        start(block, block, AG_Y + d - 1, ys[d - 1])
    start(block, block, AG_X + 0, xr)
    start(block, block, AG_X + 4, xl)
    for n, (src, dst, a, b, peer) in enumerate(halves):
        start(src.at[a], dst.at[b], HALO_K + n, peer)
    pass_chunk(0)
    every_head(own_keys, 0, 2, 4)

    level = jnp.broadcast_to(levels[...].astype(F32).reshape(1, COARSE), (CO, COARSE))
    lane = lax.broadcasted_iota(jnp.int32, (CO, COARSE), 1)
    asked = lane == t * CO + lax.broadcasted_iota(jnp.int32, (CO, COARSE), 0)
    own_level = jnp.sum(jnp.where(asked, level, 0.0), axis=1, keepdims=True)
    seen = jnp.sum(jnp.where(level <= own_level, 1.0, 0.0), axis=1, keepdims=True)
    lane = lax.broadcasted_iota(jnp.int32, (SLOTS, COARSE), 1)
    order = (lane // 128) * 128 + ((lane // 8) % 4) * 32 + ((lane // 32) % 4) * 8 + lane % 8
    allowed = order.astype(F32) < jnp.concatenate([seen] * (SLOTS // CO), axis=0)
    lmask[...] = jnp.where(allowed, 0.0, NEG)
    pass_chunk(1)

    def prepare(h, _):
        cols = head_cols(h)
        gained = cot[0:FINE, cols].astype(F32) * gain_ref[cols].reshape(1, HEAD_DIM)
        for b in range(3):
            gt[h, :, b * BLOCK : (b + 1) * BLOCK] = gained[b * BLOCK : (b + 1) * BLOCK].T
        return 0

    for d in (1, 3, 2):
        block = line(x, (y + 4 - d) % 4)
        copy(block, block, AG_Y + d - 1, ys[d - 1]).wait_recv()
        start(block, block, AG_X + d, xr)
        start(block, block, AG_X + 4 + d, xl)
    pass_chunk(2)
    every_head(own_keys, 0, 4, HEADS)
    every_head(prepare, 0, 0, HEADS)
    qd[...] = spread(tail(q)).astype(BF16)

    for d in (0, 1, 3, 2):
        yy = (y + 4 - d) % 4
        from_left, from_right = line((x + 3) % 4, yy), line((x + 1) % 4, yy)
        copy(from_left, from_left, AG_X + d, xr).wait_recv()
        if d in (0, 2):
            start(from_left, from_left, AG_F + d, xr)
        copy(from_right, from_right, AG_X + 4 + d, xl).wait_recv()
        if d in (1, 3):
            start(from_right, from_right, AG_F + d, xl)
        if d == 1:
            pass_chunk(3)
    for d in (0, 1, 3, 2):
        far = line((x + 2) % 4, (y + 4 - d) % 4)
        copy(far, far, AG_F + d, xr if d in (0, 2) else xl).wait_recv()

    def coarse_keys(h, _):
        cols = head_cols(h)
        both = cbuf[:, :, cols].astype(F32)
        keys = both[:, 0:CO].reshape(COARSE, HEAD_DIM).astype(BF16)
        values = both[:, CO:].reshape(COARSE, HEAD_DIM).astype(BF16)
        kc[:, cols] = keys
        vc[:, cols] = values
        for b in range(3):
            rows = slice(b * BLOCK, (b + 1) * BLOCK)
            scores = nt(keys, q[rows, cols]) * (SCALING * LOG2E)
            before = peaks[h, :, rows]
            peak = jnp.maximum(before, jnp.max(scores, axis=0, keepdims=True))
            weights = jnp.exp2(scores - peak)
            scale = jnp.exp2(before - peak)
            peaks[h, :, rows] = peak
            totals[h, :, rows] = totals[h, :, rows] * scale + jnp.sum(weights, axis=0, keepdims=True)
            summed[h, :, rows] = summed[h, :, rows] * scale + tn(values, weights.astype(BF16))
        return 0

    every_head(coarse_keys, 0, 0, HEADS)

    scores = nt(qd[...], kc[...]) * (SCALING * LOG2E) + lmask[...]
    peak = jnp.max(scores, axis=1, keepdims=True)
    weights = jnp.exp2(scores - peak)
    total = jnp.sum(weights, axis=1, keepdims=True)
    wide = nn(weights.astype(BF16), vc[...]) / total
    log_c = peak + jnp.log2(total)
    attended_c = collect(wide).astype(BF16).astype(F32)
    gained_c = tail(cot) * gain
    squares_c = jnp.sum(attended_c * attended_c, axis=1, keepdims=True)
    crossed_c = jnp.sum(attended_c * gained_c, axis=1, keepdims=True)

    for n, (src, dst, a, b, peer) in enumerate(halves):
        copy(src.at[a], dst.at[b], HALO_K + n, peer).wait_recv()
    for c in range(CHUNKS):
        for side in range(2):
            number, _, _, _, dst = chunk(side, c)
            copy(dst, dst, number, beside[side]).wait_recv()

    def halo_keys(h, sums):
        cols = head_cols(h)
        out = []
        for b in range(3):
            rows = slice(b * BLOCK, (b + 1) * BLOCK)
            peak = before = peaks[h, :, rows]
            scores = []
            for first, last in HALO[b]:
                part = nt(krim[first:last, cols], q[rows, cols]) * (SCALING * LOG2E)
                part = part + masked(b, first, last)
                scores.append(part)
                peak = jnp.maximum(peak, jnp.max(part, axis=0, keepdims=True))
            scale = jnp.exp2(before - peak)
            total, total_out = totals[h, :, rows] * scale, summed[h, :, rows] * scale
            for (first, last), part in zip(HALO[b], scores):
                weights = jnp.exp2(part - peak)
                total = total + jnp.sum(weights, axis=0, keepdims=True)
                total_out = total_out + tn(vrim[first:last, cols], weights.astype(BF16))
            attended = (total_out / total).astype(BF16)
            ot[h, :, rows] = attended
            logs[h, :, rows] = peak + jnp.log2(total)
            attended = attended.astype(F32)
            squares, crossed = sums[b]
            out.append((
                squares + jnp.sum(attended * attended, axis=0, keepdims=True),
                crossed + jnp.sum(attended * gt[h, :, rows], axis=0, keepdims=True),
            ))
        return tuple(out)

    sums = every_head(halo_keys, ((nothing, nothing),) * 3, 0, HEADS)

    stat[...] = jnp.zeros_like(stat)
    for b in range(3):
        stat[0:1, b * BLOCK : (b + 1) * BLOCK] = sums[b][0]
        stat[1:2, b * BLOCK : (b + 1) * BLOCK] = sums[b][1]
    stat[8:16, 0:BLOCK] = jnp.broadcast_to(squares_c, (CO, BLOCK))
    stat[8:16, BLOCK : 2 * BLOCK] = jnp.broadcast_to(crossed_c, (CO, BLOCK))
    for d in (1, 2, 3):
        start(stat, stat_in.at[d - 1], STAT + d - 1, ss[d - 1])
    for d in (1, 2, 3):
        copy(stat, stat_in.at[d - 1], STAT + d - 1, ss[d - 1]).wait_recv()
    whole = stat[...] + stat_in[0] + stat_in[1] + stat_in[2]
    inverse = lax.rsqrt(whole[0:1] / D + 1e-06)
    factor = inverse * inverse * inverse * (whole[1:2] / D)
    inverse_c = lax.rsqrt(whole[8:16, 0:1] / D + 1e-06)
    factor_c = inverse_c * inverse_c * inverse_c * (whole[8:16, BLOCK : BLOCK + 1] / D)

    normed_c = attended_c * inverse_c * gain
    grad_c = (inverse_c * gained_c - attended_c * factor_c).astype(BF16).astype(F32)
    grad_d = spread(grad_c)
    dod[...] = grad_d.astype(BF16)
    delta_c = jnp.sum(grad_d * spread(attended_c), axis=1, keepdims=True)

    def turn(h, _):
        attended = ot[h].astype(F32)
        grad = (inverse * gt[h] - attended * factor).astype(BF16)
        dot[h] = grad
        deltas[h] = jnp.sum(grad.astype(F32) * attended, axis=0, keepdims=True)
        return 0

    every_head(turn, 0, 0, HEADS)

    def back(side, h):
        return (
            BACK_V + side * HEADS + h, BACK_HOP + side * HEADS + h,
            back_out.at[side, h, 1], back_relay.at[h], back_in.at[side, h, 1],
        )

    def gradients(h, b, first, last):
        cols = head_cols(h)
        rows = slice(b * BLOCK, (b + 1) * BLOCK)
        keys, values = krim[first:last, cols], vrim[first:last, cols]
        queries, grads = q[rows, cols], dot[h, :, rows]
        scores = nt(keys, queries) * (SCALING * LOG2E) + masked(b, first, last)
        probs = jnp.exp2(scores - logs[h, :, rows])
        grad_probs = nn(values, grads)
        grad_scores = (probs * (grad_probs - deltas[h, :, rows])).astype(BF16)
        return (
            tn(keys, grad_scores), nn(grad_scores, queries) * SCALING, nt(probs.astype(BF16), grads)
        )

    def halo_grads(h, _):
        q0, k0, v0 = gradients(h, 0, 0, 192)
        q1, k1, v1 = gradients(h, 1, 128, 192)
        q2, k2, v2 = gradients(h, 1, 576, 640)
        q3, k3, v3 = gradients(h, 2, 576, 768)
        dqt[h, :, 0:BLOCK] = q0
        dqt[h, :, BLOCK : 2 * BLOCK] = q1 + q2
        dqt[h, :, 2 * BLOCK : FINE] = q3
        for n, (a, b, c, d) in enumerate(((k0, k1, k2, k3), (v0, v1, v2, v3))):
            back_out[1, h, n, 0:128] = a[0:128].astype(BF16)
            back_out[1, h, n, 128:192] = (a[128:192] + b).astype(BF16)
            back_out[0, h, n, 0:64] = (d[0:64] + c).astype(BF16)
            back_out[0, h, n, 64:192] = d[64:192].astype(BF16)
        for side in range(2):
            depart(side, *back(side, h))
            copy(
                back_out.at[side, h, 0], back_in.at[side, h, 0], BACK_K + side * HEADS + h,
                beside[side],
            ).start()
        return 0

    def pass_back(first, last):
        def body(h, _):
            for side in range(2):
                number, hop, _, via, dst = back(side, h)
                pass_on(side, number, hop, via, dst)
            return 0

        every_head(body, 0, first, last)

    every_head(halo_grads, 0, 0, HEADS)

    scores = nt(qd[...], kc[...]) * (SCALING * LOG2E) + lmask[...]
    probs = jnp.exp2(scores - log_c)
    grad_probs = nt(dod[...], vc[...])
    grad_scores = (probs * (grad_probs - delta_c)).astype(BF16)
    query_c = collect(nn(grad_scores, kc[...])) * SCALING
    coarse_row[0] = normed_c
    coarse_row[1] = query_c
    gk[...] = tn(grad_scores, qd[...])
    gv[...] = tn(probs.astype(BF16), dod[...])

    def coarse_block(j):
        rows = pl.ds(pl.multiple_of(j * BLOCK, BLOCK), BLOCK)

        def body(h, _):
            cols = head_cols(h)
            keys, values = kc[rows, cols], vc[rows, cols]
            queries, grads = q[0:FINE, cols], dot[h]
            probs = jnp.exp2(nt(keys, queries) * (SCALING * LOG2E) - logs[h])
            grad_probs = nn(values, grads)
            grad_scores = (probs * (grad_probs - deltas[h])).astype(BF16)
            gv[rows, cols] = gv[rows, cols] + nt(probs.astype(BF16), grads)
            gk[rows, cols] = (gk[rows, cols] + nn(grad_scores, queries)) * SCALING
            part = tn(keys, grad_scores)
            dqt[h] = dqt[h] + part
            return 0

        every_head(body, 0, 0, HEADS)
        return rows

    rows = coarse_block((x + 2) % 4)
    opp_out[0] = gk[rows].astype(BF16)
    opp_out[1] = gv[rows].astype(BF16)
    start(opp_out.at[0], opp_in.at[0], RS_OPP, xr)
    start(opp_out.at[1], opp_in.at[1], RS_OPP + 1, xl)
    pass_back(0, 2)
    rows_r = coarse_block((x + 1) % 4)
    pass_back(2, 4)
    rows_l = coarse_block((x + 3) % 4)
    copy(opp_out.at[0], opp_in.at[0], RS_OPP, xr).wait_recv()
    x_out[0] = (gk[rows_r] + opp_in[0].astype(F32)).astype(BF16)
    x_out[1] = gv[rows_r].astype(BF16)
    start(x_out.at[0], x_in.at[0], RS_X, xr)
    start(x_out.at[1], x_in.at[1], RS_X + 1, xr)
    copy(opp_out.at[1], opp_in.at[1], RS_OPP + 1, xl).wait_recv()
    x_out[2] = gk[rows_l].astype(BF16)
    x_out[3] = (gv[rows_l] + opp_in[1].astype(F32)).astype(BF16)
    start(x_out.at[2], x_in.at[2], RS_X + 2, xl)
    start(x_out.at[3], x_in.at[3], RS_X + 3, xl)
    pass_back(4, 6)

    own = coarse_block(x)
    pass_back(6, 7)

    def own_grads(h, _):
        for b in range(3):
            first, last = OWN[b]
            part, part_k, part_v = gradients(h, b, first, last)
            rows = slice(b * BLOCK, (b + 1) * BLOCK)
            dqt[h, :, rows] = dqt[h, :, rows] + part
            here = slice(first - WIN, last - WIN)
            if b == 0:
                own_k[h, here], own_v[h, here] = part_k, part_v
                rest = slice(last - WIN, FINE)
                own_k[h, rest] = jnp.zeros((FINE + WIN - last, HEAD_DIM), F32)
                own_v[h, rest] = jnp.zeros((FINE + WIN - last, HEAD_DIM), F32)
            else:
                own_k[h, here] = own_k[h, here] + part_k
                own_v[h, here] = own_v[h, here] + part_v
        return 0

    every_head(own_grads, 0, 0, HEADS)

    for n in range(4):
        copy(x_out.at[n], x_in.at[n], RS_X + n, xr if n < 2 else xl).wait_recv()
    gk[own] = gk[own] + x_in[0].astype(F32) + x_in[2].astype(F32)
    gv[own] = gv[own] + x_in[1].astype(F32) + x_in[3].astype(F32)

    def piece(yy, zz, size):
        return pl.ds(pl.multiple_of(x * 128 + yy * 32 + zz * CO, size), size)

    for d in (1, 2, 3):
        there = piece((y + d) % 4, 0, 32)
        y_out[d - 1, 0] = gk[there].astype(BF16)
        y_out[d - 1, 1] = gv[there].astype(BF16)
        start(y_out.at[d - 1], y_in.at[d - 1], RS_Y + d - 1, ys[d - 1])

    def finish(h, _):
        cols = head_cols(h)
        own_gain = gain_ref[cols].reshape(1, HEAD_DIM)
        queries, normed = [], []
        for b in range(3):
            rows = slice(b * BLOCK, (b + 1) * BLOCK)
            queries.append((dqt[h, :, rows] * SCALING).T)
            normed.append((ot[h, :, rows].astype(F32) * inverse[:, rows]).T * own_gain)
        of_n[:, cols] = jnp.concatenate(normed + [coarse_row[0, :, cols]], axis=0).astype(BF16)
        of_q[:, cols] = jnp.concatenate(queries + [coarse_row[1, :, cols]], axis=0).astype(BF16)
        return 0

    every_head(finish, 0, 0, HEADS)

    for d in (1, 2, 3):
        copy(y_out.at[d - 1], y_in.at[d - 1], RS_Y + d - 1, ys[d - 1]).wait_recv()
    here = piece(y, 0, 32)
    for n, total in enumerate((gk, gv)):
        total[here] = (
            total[here]
            + y_in[0, n].astype(F32) + y_in[1, n].astype(F32) + y_in[2, n].astype(F32)
        )
    for d in (1, 2, 3):
        there = piece(y, (z + d) % 4, CO)
        z_out[d - 1, 0] = gk[there]
        z_out[d - 1, 1] = gv[there]
        start(z_out.at[d - 1], z_in.at[d - 1], RS_Z + d - 1, zs[d - 1])
    for d in (1, 2, 3):
        copy(z_out.at[d - 1], z_in.at[d - 1], RS_Z + d - 1, zs[d - 1]).wait_recv()
    here = piece(y, z, CO)
    coarse_row[0] = gk[here] + z_in[0, 0] + z_in[1, 0] + z_in[2, 0]
    coarse_row[1] = gv[here] + z_in[0, 1] + z_in[1, 1] + z_in[2, 1]

    def fold(h, _):
        cols = head_cols(h)
        for side in range(2):
            number, hop, src, _, dst = back(side, h)
            copy(dst, dst, number, beside[side]).wait_recv()
            departed(side, number, hop, src)
            copy(
                back_out.at[side, h, 0], back_in.at[side, h, 0], BACK_K + side * HEADS + h,
                beside[side],
            ).wait()
        for n, (mine, target) in enumerate(((own_k, of_k), (own_v, of_v))):
            parts = [
                mine[h, side * WIN : (side + 1) * WIN] + back_in[side, h, n].astype(F32)
                for side in range(2)
            ]
            target[:, cols] = jnp.concatenate(
                parts + [coarse_row[n, :, cols]], axis=0
            ).astype(BF16)
        return 0

    every_head(fold, 0, 0, HEADS)
    for c in range(CHUNKS):
        for side in range(2):
            number, hop, src, _, _ = chunk(side, c)
            departed(side, number, hop, src)
    for c in pending:
        c.wait_send()


def deliver(a, b, c, d, to_a, to_b, to_c, to_d, held, arrive, leave):
    pairs = ((a, to_a), (b, to_b), (c, to_c), (d, to_d))
    inward = [pltpu.make_async_copy(p[0], held.at[n], arrive.at[n]) for n, p in enumerate(pairs)]
    outward = [pltpu.make_async_copy(held.at[n], p[1], leave.at[n]) for n, p in enumerate(pairs)]
    for c in inward:
        c.start()
    for n in range(4):
        inward[n].wait()
        outward[n].start()
    for c in outward:
        c.wait()


def on_device(query_rows, key_rows, value_rows, scale_index, norm_gain, cotangent):
    full = jax.ShapeDtypeStruct((FINE + CO, COLS), BF16)
    whole = pl.BlockSpec(memory_space=pltpu.VMEM)
    scratch = [
        pltpu.VMEM((RIM, COLS), BF16),
        pltpu.VMEM((RIM, COLS), BF16),
        pltpu.VMEM((64, 16, COLS), BF16),
        pltpu.VMEM((COARSE, COLS), BF16),
        pltpu.VMEM((COARSE, COLS), BF16),
        pltpu.VMEM((3, SPAN, BLOCK), F32),
        pltpu.VMEM((SLOTS, COARSE), F32),
        pltpu.VMEM((HEADS, HEAD_DIM, FINE), F32),
        pltpu.VMEM((HEADS, HEAD_DIM, FINE), BF16),
        pltpu.VMEM((HEADS, HEAD_DIM, FINE), BF16),
        pltpu.VMEM((HEADS, 1, FINE), F32),
        pltpu.VMEM((HEADS, 1, FINE), F32),
        pltpu.VMEM((HEADS, HEAD_DIM, FINE), F32),
        pltpu.VMEM((16, FINE), F32),
        pltpu.VMEM((3, 16, FINE), F32),
        pltpu.VMEM((2, CO, COLS), F32),
        pltpu.VMEM((SLOTS, COLS), BF16),
        pltpu.VMEM((SLOTS, COLS), BF16),
        pltpu.VMEM((COARSE, COLS), F32),
        pltpu.VMEM((COARSE, COLS), F32),
        pltpu.VMEM((HEADS, 1, FINE), F32),
        pltpu.VMEM((HEADS, 1, FINE), F32),
        pltpu.VMEM((HEADS, HEAD_DIM, FINE), F32),
        pltpu.VMEM((HEADS, FINE, HEAD_DIM), F32),
        pltpu.VMEM((HEADS, FINE, HEAD_DIM), F32),
        pltpu.VMEM((2, BLOCK, COLS), BF16),
        pltpu.VMEM((2, BLOCK, COLS), BF16),
        pltpu.VMEM((4, BLOCK, COLS), BF16),
        pltpu.VMEM((4, BLOCK, COLS), BF16),
        pltpu.VMEM((3, 2, 32, COLS), BF16),
        pltpu.VMEM((3, 2, 32, COLS), BF16),
        pltpu.VMEM((3, 2, CO, COLS), F32),
        pltpu.VMEM((3, 2, CO, COLS), F32),
        pltpu.VMEM((2, HEADS, 2, WIN, HEAD_DIM), BF16),
        pltpu.VMEM((2, HEADS, 2, WIN, HEAD_DIM), BF16),
        pltpu.VMEM((CHUNKS, CHUNK, COLS), BF16),
        pltpu.VMEM((HEADS, WIN, HEAD_DIM), BF16),
        pltpu.SemaphoreType.DMA((COPIES,)),
        pltpu.SemaphoreType.DMA((COPIES,)),
    ]
    results = pl.pallas_call(
        kernel,
        out_shape=[full] * 4,
        in_specs=[whole] * 6,
        out_specs=[whole] * 4,
        scratch_shapes=scratch,
        compiler_params=pltpu.CompilerParams(
            collective_id=0, has_side_effects=True, vmem_limit_bytes=56 * 1024 * 1024
        ),
    )(query_rows, key_rows, value_rows, cotangent, norm_gain, scale_index)
    anywhere = pl.BlockSpec(memory_space=pl.ANY)
    return tuple(pl.pallas_call(
        deliver,
        out_shape=[full] * 4,
        in_specs=[anywhere] * 4,
        out_specs=[anywhere] * 4,
        scratch_shapes=[
            pltpu.VMEM((4, FINE + CO, COLS), BF16),
            pltpu.SemaphoreType.DMA((4,)),
            pltpu.SemaphoreType.DMA((4,)),
        ],
    )(*results))


def solution(mesh):
    both = P("space", "scale")
    return jax.shard_map(
        on_device, mesh=mesh, in_specs=(both, both, both, P(), P("scale"), both),
        out_specs=(both, both, both, both), check_vma=False,
    )
```

```python
import jax
import jax.numpy as jnp
from jax import lax
from jax.experimental import pallas as pl
from jax.experimental.pallas import tpu as pltpu
from jax.sharding import PartitionSpec as P

HEAD_DIM = 128
HEADS = 7
COLS = HEADS * HEAD_DIM
D = 3584
FINE = 384
WIN = 192
RIM = FINE + 2 * WIN
CO = 8
COARSE = 512
LEVELS = 6
SLOTS = 128
BLOCK = 128
SPAN = 512
OWN = ((192, 512), (192, 576), (256, 576))
HALO = (((0, 192),), ((128, 192), (576, 640)), ((576, 768),))
NEG = -1e30
SCALING = HEAD_DIM ** (-0.5)
LOG2E = 1.4426950408889634
LN2 = 0.6931471805599453
F32 = jnp.float32
BF16 = jnp.bfloat16
MESH = pl.DeviceIdType.MESH

CHUNKS = 4
CHUNK = WIN // CHUNKS
HALF = WIN // 2
EARLY = (0, 1)
HALO_K = 0
HALO_V = HALO_K + 4
HOP = HALO_V + 2 * CHUNKS
AG_Z = HOP + 2 * CHUNKS
AG_Y = AG_Z + 3
AG_X = AG_Y + 3
AG_F = AG_X + 8
STAT = AG_F + 4
RS_OPP = STAT + 3
RS_X = RS_OPP + 2
RS_Y = RS_X + 4
RS_Z = RS_Y + 3
BACK_K = RS_Z + 3
BACK_V = BACK_K + 2 * HEADS
BACK_HOP = BACK_V + 2 * HEADS
COPIES = BACK_HOP + 2 * HEADS


def nt(a, b):
    return lax.dot_general(a, b, (((1,), (1,)), ((), ())), preferred_element_type=F32)


def nn(a, b):
    return lax.dot_general(a, b, (((1,), (0,)), ((), ())), preferred_element_type=F32)


def tn(a, b):
    return lax.dot_general(a, b, (((0,), (0,)), ((), ())), preferred_element_type=F32)


def every_head(body, carry=0, first=0, last=HEADS):
    for h in range(first, last):
        carry = body(h, carry)
    return carry


def head_cols(h):
    if isinstance(h, int):
        return slice(h * HEAD_DIM, (h + 1) * HEAD_DIM)
    return pl.ds(pl.multiple_of(h * HEAD_DIM, HEAD_DIM), HEAD_DIM)


def diagonal(rows):
    slot = lax.broadcasted_iota(jnp.int32, (rows, COLS), 0) // CO
    column = lax.broadcasted_iota(jnp.int32, (rows, COLS), 1) // HEAD_DIM
    return slot == column


def spread(piece):
    return jnp.where(diagonal(SLOTS), jnp.concatenate([piece] * (SLOTS // CO), axis=0), 0.0)


def collect(wide):
    kept = jnp.where(diagonal(SLOTS), wide, 0.0)
    total = kept[0:CO]
    for g in range(1, HEADS):
        total = total + kept[g * CO : (g + 1) * CO]
    return total


def kernel(
    q, k, v, cot, gain_ref, levels,
    of_n, of_q, of_k, of_v,
    krim, vrim, cbuf, kc, vc, masks, lmask, gt, ot, dot, logs, deltas, dqt,
    stat, stat_in, coarse_row, qd, dod, gk, gv, peaks, totals, summed, own_k, own_v,
    opp_out, opp_in, x_out, x_in, y_out, y_in, z_out, z_in, back_out, back_in,
    relay, back_relay, send, recv,
):
    t = lax.axis_index("space")
    s = lax.axis_index("scale")
    x, z, y = t // 16, (t // 4) % 4, t % 4

    def at(xx, zz, yy):
        return {"space": xx * 16 + zz * 4 + yy}

    right = {"space": (t + 1) % 64}
    left = {"space": (t + 63) % 64}
    xr, xl = at((x + 1) % 4, z, y), at((x + 3) % 4, z, y)
    ys = [at(x, z, (y + d) % 4) for d in (1, 2, 3)]
    zs = [at(x, (z + d) % 4, y) for d in (1, 2, 3)]
    ss = [{"scale": (s + d) % 4} for d in (1, 2, 3)]
    carry = [at((x + 1) % 4, (z + 1) % 4, y), at((x + 3) % 4, (z + 3) % 4, y)]

    edges = (y == 3, y == 0)
    relaying = (y == 0, y == 3)
    beside = (right, left)
    first_hop = (at(x, z, 0), at(x, z, 3))
    last_hop = (
        at((x + jnp.where(z == 3, 1, 0)) % 4, (z + 1) % 4, 0),
        at((x + jnp.where(z == 0, 3, 0)) % 4, (z + 3) % 4, 3),
    )

    def copy(src, dst, number, peer, out_number=None):
        return pltpu.make_async_remote_copy(
            src_ref=src, dst_ref=dst,
            send_sem=send.at[number if out_number is None else out_number],
            recv_sem=recv.at[number], device_id=peer, device_id_type=MESH,
        )

    pending = []

    def start(src, dst, number, peer):
        c = copy(src, dst, number, peer)
        c.start()
        pending.append(c)

    def depart_edge(side, number, hop, src, via, dst):
        @pl.when(edges[side])
        def _():
            copy(src, via, hop, first_hop[side]).start()

    def depart_inner(side, number, hop, src, via, dst):
        @pl.when(jnp.logical_not(edges[side]))
        def _():
            copy(src, dst, number, beside[side]).start()

    def depart(*transfer):
        depart_edge(*transfer)
        depart_inner(*transfer)

    def pass_on(side, number, hop, via, dst):
        @pl.when(relaying[side])
        def _():
            copy(via, via, hop, first_hop[side]).wait_recv()
            copy(via, dst, number, last_hop[side], hop).start()

    def departed(side, number, hop, src):
        @pl.when(edges[side] | relaying[side])
        def _():
            copy(src, src, hop, beside[side]).wait_send()

        @pl.when(jnp.logical_not(edges[side]))
        def _():
            copy(src, src, number, beside[side]).wait_send()

    barrier = pltpu.get_barrier_semaphore()
    greeted = [left, right, xl, xr] + ys + zs + ss + carry
    for peer in greeted:
        pl.semaphore_signal(barrier, inc=1, device_id=peer, device_id_type=MESH)

    def tail(ref):
        return ref[...].astype(F32)[FINE:]

    gain = gain_ref[...].reshape(1, COLS)
    mine = x * 16 + y * 4 + z
    cbuf[mine] = jnp.concatenate([tail(k), tail(v)], axis=0).astype(BF16)
    pl.semaphore_wait(barrier, len(greeted))

    for d in (1, 2, 3):
        start(cbuf.at[mine], cbuf.at[mine], AG_Z + d - 1, zs[d - 1])

    def chunk(side, c):
        a = c * CHUNK + (WIN if side == 0 else 0)
        b = c * CHUNK + (0 if side == 0 else WIN + FINE)
        return (
            HALO_V + side * CHUNKS + c, HOP + side * CHUNKS + c,
            v.at[a : a + CHUNK], relay.at[c], vrim.at[b : b + CHUNK],
        )

    for c in EARLY:
        for side in range(2):
            depart_edge(side, *chunk(side, c))
    halves = (
        (k, krim, slice(WIN, WIN + HALF), slice(0, HALF), right),
        (k, krim, slice(0, HALF), slice(WIN + FINE, WIN + FINE + HALF), left),
        (k, krim, slice(WIN + HALF, 2 * WIN), slice(HALF, WIN), right),
        (k, krim, slice(HALF, WIN), slice(WIN + FINE + HALF, RIM), left),
    )

    def send_keys(n, when):
        src, dst, a, b, peer = halves[n]

        @pl.when(when)
        def _():
            copy(src.at[a], dst.at[b], HALO_K + n, peer).start()

    def pass_chunk(c):
        for side in range(2):
            number, hop, _, via, dst = chunk(side, c)
            pass_on(side, number, hop, via, dst)

    def line(xx, yy):
        return cbuf.at[pl.ds(xx * 16 + yy * 4, 4)]

    krim[WIN : WIN + FINE] = k[0:FINE]
    vrim[WIN : WIN + FINE] = v[0:FINE]
    row = lax.broadcasted_iota(jnp.int32, (SPAN, BLOCK), 0)
    column = lax.broadcasted_iota(jnp.int32, (SPAN, BLOCK), 1)
    for b in range(3):
        near = (row >= column) & (row - column <= 2 * WIN)
        place = row + b * BLOCK
        here = ((place >= WIN) | (t > 0)) & ((place < WIN + FINE) | (t < 63))
        masks[b] = jnp.where(near & here, 0.0, NEG)

    nothing = jnp.zeros((1, BLOCK), F32)

    def masked(b, first, last):
        return masks[b, first - b * BLOCK : last - b * BLOCK]

    def own_keys(h, _):
        cols = head_cols(h)
        for b in range(3):
            rows = slice(b * BLOCK, (b + 1) * BLOCK)
            first, last = OWN[b]
            scores = nt(krim[first:last, cols], q[rows, cols]) * (SCALING * LOG2E)
            scores = scores + masked(b, first, last)
            peak = jnp.max(scores, axis=0, keepdims=True)
            weights = jnp.exp2(scores - peak)
            peaks[h, :, rows] = peak
            totals[h, :, rows] = jnp.sum(weights, axis=0, keepdims=True)
            summed[h, :, rows] = tn(vrim[first:last, cols], weights.astype(BF16))
        return 0

    every_head(own_keys, 0, 0, 2)
    for d in (1, 3, 2):
        got = cbuf.at[x * 16 + y * 4 + (z + 4 - d) % 4]
        copy(got, got, AG_Z + d - 1, zs[d - 1]).wait_recv()
    block = line(x, y)
    for d in (1, 3, 2):
        start(block, block, AG_Y + d - 1, ys[d - 1])
    start(block, block, AG_X + 0, xr)
    start(block, block, AG_X + 4, xl)
    pass_chunk(0)
    pass_chunk(1)
    every_head(own_keys, 0, 2, 4)

    level = jnp.broadcast_to(levels[...].astype(F32).reshape(1, COARSE), (CO, COARSE))
    lane = lax.broadcasted_iota(jnp.int32, (CO, COARSE), 1)
    asked = lane == t * CO + lax.broadcasted_iota(jnp.int32, (CO, COARSE), 0)
    own_level = jnp.sum(jnp.where(asked, level, 0.0), axis=1, keepdims=True)
    seen = jnp.sum(jnp.where(level <= own_level, 1.0, 0.0), axis=1, keepdims=True)
    lane = lax.broadcasted_iota(jnp.int32, (SLOTS, COARSE), 1)
    order = (lane // 128) * 128 + ((lane // 8) % 4) * 32 + ((lane // 32) % 4) * 8 + lane % 8
    allowed = order.astype(F32) < jnp.concatenate([seen] * (SLOTS // CO), axis=0)
    lmask[...] = jnp.where(allowed, 0.0, NEG)

    def prepare(h, _):
        cols = head_cols(h)
        gained = cot[0:FINE, cols].astype(F32) * gain_ref[cols].reshape(1, HEAD_DIM)
        for b in range(3):
            gt[h, :, b * BLOCK : (b + 1) * BLOCK] = gained[b * BLOCK : (b + 1) * BLOCK].T
        return 0

    for d in (1, 3, 2):
        block = line(x, (y + 4 - d) % 4)
        copy(block, block, AG_Y + d - 1, ys[d - 1]).wait_recv()
        start(block, block, AG_X + d, xr)
        start(block, block, AG_X + 4 + d, xl)
    for c in range(CHUNKS):
        for side in range(2):
            if c in EARLY:
                depart_inner(side, *chunk(side, c))
            else:
                depart(side, *chunk(side, c))
    for n in range(4):
        send_keys(n, y >= 0)
    every_head(own_keys, 0, 4, HEADS)
    every_head(prepare, 0, 0, HEADS)
    qd[...] = spread(tail(q)).astype(BF16)

    for d in (0, 1, 3, 2):
        yy = (y + 4 - d) % 4
        from_left, from_right = line((x + 3) % 4, yy), line((x + 1) % 4, yy)
        copy(from_left, from_left, AG_X + d, xr).wait_recv()
        if d in (0, 2):
            start(from_left, from_left, AG_F + d, xr)
        copy(from_right, from_right, AG_X + 4 + d, xl).wait_recv()
        if d in (1, 3):
            start(from_right, from_right, AG_F + d, xl)
        if d in (0, 1):
            pass_chunk(2 + d)
    for d in (0, 1, 3, 2):
        far = line((x + 2) % 4, (y + 4 - d) % 4)
        copy(far, far, AG_F + d, xr if d in (0, 2) else xl).wait_recv()

    def coarse_keys(h, _):
        cols = head_cols(h)
        both = cbuf[:, :, cols].astype(F32)
        keys = both[:, 0:CO].reshape(COARSE, HEAD_DIM).astype(BF16)
        values = both[:, CO:].reshape(COARSE, HEAD_DIM).astype(BF16)
        kc[:, cols] = keys
        vc[:, cols] = values
        for b in range(3):
            rows = slice(b * BLOCK, (b + 1) * BLOCK)
            scores = nt(keys, q[rows, cols]) * (SCALING * LOG2E)
            before = peaks[h, :, rows]
            peak = jnp.maximum(before, jnp.max(scores, axis=0, keepdims=True))
            weights = jnp.exp2(scores - peak)
            scale = jnp.exp2(before - peak)
            peaks[h, :, rows] = peak
            totals[h, :, rows] = totals[h, :, rows] * scale + jnp.sum(weights, axis=0, keepdims=True)
            summed[h, :, rows] = summed[h, :, rows] * scale + tn(values, weights.astype(BF16))
        return 0

    every_head(coarse_keys, 0, 0, HEADS)

    scores = nt(qd[...], kc[...]) * (SCALING * LOG2E) + lmask[...]
    peak = jnp.max(scores, axis=1, keepdims=True)
    weights = jnp.exp2(scores - peak)
    total = jnp.sum(weights, axis=1, keepdims=True)
    wide = nn(weights.astype(BF16), vc[...]) / total
    log_c = peak + jnp.log2(total)
    attended_c = collect(wide).astype(BF16).astype(F32)
    gained_c = tail(cot) * gain
    squares_c = jnp.sum(attended_c * attended_c, axis=1, keepdims=True)
    crossed_c = jnp.sum(attended_c * gained_c, axis=1, keepdims=True)

    for n, (src, dst, a, b, peer) in enumerate(halves):
        copy(src.at[a], dst.at[b], HALO_K + n, peer).wait()
    for c in range(CHUNKS):
        for side in range(2):
            number, _, _, _, dst = chunk(side, c)
            copy(dst, dst, number, beside[side]).wait_recv()

    def halo_keys(h, sums):
        cols = head_cols(h)
        out = []
        for b in range(3):
            rows = slice(b * BLOCK, (b + 1) * BLOCK)
            peak = before = peaks[h, :, rows]
            scores = []
            for first, last in HALO[b]:
                part = nt(krim[first:last, cols], q[rows, cols]) * (SCALING * LOG2E)
                part = part + masked(b, first, last)
                scores.append(part)
                peak = jnp.maximum(peak, jnp.max(part, axis=0, keepdims=True))
            scale = jnp.exp2(before - peak)
            total, total_out = totals[h, :, rows] * scale, summed[h, :, rows] * scale
            for (first, last), part in zip(HALO[b], scores):
                weights = jnp.exp2(part - peak)
                total = total + jnp.sum(weights, axis=0, keepdims=True)
                total_out = total_out + tn(vrim[first:last, cols], weights.astype(BF16))
            attended = (total_out / total).astype(BF16)
            ot[h, :, rows] = attended
            logs[h, :, rows] = peak + jnp.log2(total)
            attended = attended.astype(F32)
            squares, crossed = sums[b]
            out.append((
                squares + jnp.sum(attended * attended, axis=0, keepdims=True),
                crossed + jnp.sum(attended * gt[h, :, rows], axis=0, keepdims=True),
            ))
        return tuple(out)

    sums = every_head(halo_keys, ((nothing, nothing),) * 3, 0, HEADS)

    stat[...] = jnp.zeros_like(stat)
    for b in range(3):
        stat[0:1, b * BLOCK : (b + 1) * BLOCK] = sums[b][0]
        stat[1:2, b * BLOCK : (b + 1) * BLOCK] = sums[b][1]
    stat[8:16, 0:BLOCK] = jnp.broadcast_to(squares_c, (CO, BLOCK))
    stat[8:16, BLOCK : 2 * BLOCK] = jnp.broadcast_to(crossed_c, (CO, BLOCK))
    for d in (1, 2, 3):
        start(stat, stat_in.at[d - 1], STAT + d - 1, ss[d - 1])
    for d in (1, 2, 3):
        copy(stat, stat_in.at[d - 1], STAT + d - 1, ss[d - 1]).wait_recv()
    whole = stat[...] + stat_in[0] + stat_in[1] + stat_in[2]
    inverse = lax.rsqrt(whole[0:1] / D + 1e-06)
    factor = inverse * inverse * inverse * (whole[1:2] / D)
    inverse_c = lax.rsqrt(whole[8:16, 0:1] / D + 1e-06)
    factor_c = inverse_c * inverse_c * inverse_c * (whole[8:16, BLOCK : BLOCK + 1] / D)

    normed_c = attended_c * inverse_c * gain
    grad_c = (inverse_c * gained_c - attended_c * factor_c).astype(BF16).astype(F32)
    grad_d = spread(grad_c)
    dod[...] = grad_d.astype(BF16)
    delta_c = jnp.sum(grad_d * spread(attended_c), axis=1, keepdims=True)

    def turn(h, _):
        attended = ot[h].astype(F32)
        grad = (inverse * gt[h] - attended * factor).astype(BF16)
        dot[h] = grad
        deltas[h] = jnp.sum(grad.astype(F32) * attended, axis=0, keepdims=True)
        return 0

    every_head(turn, 0, 0, HEADS)

    def back(side, h):
        return (
            BACK_V + side * HEADS + h, BACK_HOP + side * HEADS + h,
            back_out.at[side, h, 1], back_relay.at[h], back_in.at[side, h, 1],
        )

    def gradients(h, b, first, last):
        cols = head_cols(h)
        rows = slice(b * BLOCK, (b + 1) * BLOCK)
        keys, values = krim[first:last, cols], vrim[first:last, cols]
        queries, grads = q[rows, cols], dot[h, :, rows]
        scores = nt(keys, queries) * (SCALING * LOG2E) + masked(b, first, last)
        probs = jnp.exp2(scores - logs[h, :, rows])
        grad_probs = nn(values, grads)
        grad_scores = (probs * (grad_probs - deltas[h, :, rows])).astype(BF16)
        return (
            tn(keys, grad_scores), nn(grad_scores, queries) * SCALING, nt(probs.astype(BF16), grads)
        )

    def halo_grads(h, _):
        q0, k0, v0 = gradients(h, 0, 0, 192)
        q1, k1, v1 = gradients(h, 1, 128, 192)
        q2, k2, v2 = gradients(h, 1, 576, 640)
        q3, k3, v3 = gradients(h, 2, 576, 768)
        dqt[h] = jnp.concatenate([q0, q1 + q2, q3], axis=1)
        for n, (a, b, c, d) in enumerate(((k0, k1, k2, k3), (v0, v1, v2, v3))):
            back_out[1, h, n, 0:128] = a[0:128].astype(BF16)
            back_out[1, h, n, 128:192] = (a[128:192] + b).astype(BF16)
            back_out[0, h, n, 0:64] = (d[0:64] + c).astype(BF16)
            back_out[0, h, n, 64:192] = d[64:192].astype(BF16)
        for side in range(2):
            depart(side, *back(side, h))
            copy(
                back_out.at[side, h, 0], back_in.at[side, h, 0], BACK_K + side * HEADS + h,
                beside[side],
            ).start()
        return 0

    def pass_back(first, last):
        def body(h, _):
            for side in range(2):
                number, hop, _, via, dst = back(side, h)
                pass_on(side, number, hop, via, dst)
            return 0

        every_head(body, 0, first, last)

    every_head(halo_grads, 0, 0, HEADS)

    scores = nt(qd[...], kc[...]) * (SCALING * LOG2E) + lmask[...]
    probs = jnp.exp2(scores - log_c)
    grad_probs = nt(dod[...], vc[...])
    grad_scores = (probs * (grad_probs - delta_c)).astype(BF16)
    query_c = collect(nn(grad_scores, kc[...])) * SCALING
    coarse_row[0] = normed_c
    coarse_row[1] = query_c
    gk[...] = tn(grad_scores, qd[...])
    gv[...] = tn(probs.astype(BF16), dod[...])

    def coarse_block(j):
        rows = pl.ds(pl.multiple_of(j * BLOCK, BLOCK), BLOCK)

        def body(h, _):
            cols = head_cols(h)
            keys, values = kc[rows, cols], vc[rows, cols]
            queries, grads = q[0:FINE, cols], dot[h]
            probs = jnp.exp2(nt(keys, queries) * (SCALING * LOG2E) - logs[h])
            grad_probs = nn(values, grads)
            grad_scores = (probs * (grad_probs - deltas[h])).astype(BF16)
            gv[rows, cols] = gv[rows, cols] + nt(probs.astype(BF16), grads)
            gk[rows, cols] = (gk[rows, cols] + nn(grad_scores, queries)) * SCALING
            part = tn(keys, grad_scores)
            dqt[h] = dqt[h] + part
            return 0

        every_head(body, 0, 0, HEADS)
        return rows

    rows = coarse_block((x + 2) % 4)
    opp_out[0] = gk[rows].astype(BF16)
    opp_out[1] = gv[rows].astype(BF16)
    start(opp_out.at[0], opp_in.at[0], RS_OPP, xr)
    start(opp_out.at[1], opp_in.at[1], RS_OPP + 1, xl)
    pass_back(0, 3)
    rows_r = coarse_block((x + 1) % 4)
    copy(opp_out.at[0], opp_in.at[0], RS_OPP, xr).wait_recv()
    x_out[0] = (gk[rows_r] + opp_in[0].astype(F32)).astype(BF16)
    x_out[1] = gv[rows_r].astype(BF16)
    start(x_out.at[0], x_in.at[0], RS_X, xr)
    start(x_out.at[1], x_in.at[1], RS_X + 1, xr)
    pass_back(3, 4)
    rows_l = coarse_block((x + 3) % 4)
    copy(opp_out.at[1], opp_in.at[1], RS_OPP + 1, xl).wait_recv()
    x_out[2] = gk[rows_l].astype(BF16)
    x_out[3] = (gv[rows_l] + opp_in[1].astype(F32)).astype(BF16)
    start(x_out.at[2], x_in.at[2], RS_X + 2, xl)
    start(x_out.at[3], x_in.at[3], RS_X + 3, xl)
    pass_back(4, 5)
    own = coarse_block(x)
    pass_back(5, 6)

    def own_grads(h, _):
        for b in range(3):
            first, last = OWN[b]
            part, part_k, part_v = gradients(h, b, first, last)
            rows = slice(b * BLOCK, (b + 1) * BLOCK)
            dqt[h, :, rows] = dqt[h, :, rows] + part
            here = slice(first - WIN, last - WIN)
            if b == 0:
                own_k[h, here], own_v[h, here] = part_k, part_v
                rest = slice(last - WIN, FINE)
                own_k[h, rest] = jnp.zeros((FINE + WIN - last, HEAD_DIM), F32)
                own_v[h, rest] = jnp.zeros((FINE + WIN - last, HEAD_DIM), F32)
            else:
                own_k[h, here] = own_k[h, here] + part_k
                own_v[h, here] = own_v[h, here] + part_v
        return 0

    every_head(own_grads, 0, 0, HEADS)
    pass_back(6, 7)

    for n in range(4):
        copy(x_out.at[n], x_in.at[n], RS_X + n, xr if n < 2 else xl).wait_recv()
    gk[own] = gk[own] + x_in[0].astype(F32) + x_in[2].astype(F32)
    gv[own] = gv[own] + x_in[1].astype(F32) + x_in[3].astype(F32)

    def piece(yy, zz, size):
        return pl.ds(pl.multiple_of(x * 128 + yy * 32 + zz * CO, size), size)

    for d in (1, 2, 3):
        there = piece((y + d) % 4, 0, 32)
        y_out[d - 1, 0] = gk[there].astype(BF16)
        y_out[d - 1, 1] = gv[there].astype(BF16)
        start(y_out.at[d - 1], y_in.at[d - 1], RS_Y + d - 1, ys[d - 1])

    def finish(h, _):
        cols = head_cols(h)
        own_gain = gain_ref[cols].reshape(1, HEAD_DIM)
        queries, normed = [], []
        for b in range(3):
            rows = slice(b * BLOCK, (b + 1) * BLOCK)
            queries.append((dqt[h, :, rows] * SCALING).T)
            normed.append((ot[h, :, rows].astype(F32) * inverse[:, rows]).T * own_gain)
        of_n[:, cols] = jnp.concatenate(normed + [coarse_row[0, :, cols]], axis=0).astype(BF16)
        of_q[:, cols] = jnp.concatenate(queries + [coarse_row[1, :, cols]], axis=0).astype(BF16)
        return 0


    every_head(finish, 0, 0, HEADS)
    for d in (1, 2, 3):
        copy(y_out.at[d - 1], y_in.at[d - 1], RS_Y + d - 1, ys[d - 1]).wait_recv()
    here = piece(y, 0, 32)
    for n, total in enumerate((gk, gv)):
        total[here] = (
            total[here]
            + y_in[0, n].astype(F32) + y_in[1, n].astype(F32) + y_in[2, n].astype(F32)
        )
    for d in (1, 2, 3):
        there = piece(y, (z + d) % 4, CO)
        z_out[d - 1] = jnp.concatenate([gk[there], gv[there]], axis=0).astype(BF16)
        start(z_out.at[d - 1], z_in.at[d - 1], RS_Z + d - 1, zs[d - 1])
    for d in (1, 2, 3):
        copy(z_out.at[d - 1], z_in.at[d - 1], RS_Z + d - 1, zs[d - 1]).wait_recv()
    here = piece(y, z, CO)
    arrived = z_in[0].astype(F32) + z_in[1].astype(F32) + z_in[2].astype(F32)
    coarse_row[0] = gk[here] + arrived[0:CO]
    coarse_row[1] = gv[here] + arrived[CO:]

    def fold(h, _):
        cols = head_cols(h)
        for side in range(2):
            number, hop, src, _, dst = back(side, h)
            copy(dst, dst, number, beside[side]).wait_recv()
            departed(side, number, hop, src)
            copy(
                back_out.at[side, h, 0], back_in.at[side, h, 0], BACK_K + side * HEADS + h,
                beside[side],
            ).wait()
        for n, (mine, target) in enumerate(((own_k, of_k), (own_v, of_v))):
            parts = [
                mine[h, side * WIN : (side + 1) * WIN] + back_in[side, h, n].astype(F32)
                for side in range(2)
            ]
            target[:, cols] = jnp.concatenate(
                parts + [coarse_row[n, :, cols]], axis=0
            ).astype(BF16)
        return 0

    every_head(fold, 0, 0, HEADS)
    for c in range(CHUNKS):
        for side in range(2):
            number, hop, src, _, _ = chunk(side, c)
            departed(side, number, hop, src)
    for c in pending:
        c.wait_send()


def deliver(a, b, c, d, to_a, to_b, to_c, to_d, held, arrive, leave):
    pairs = ((a, to_a), (b, to_b), (c, to_c), (d, to_d))
    inward = [pltpu.make_async_copy(p[0], held.at[n], arrive.at[n]) for n, p in enumerate(pairs)]
    outward = [pltpu.make_async_copy(held.at[n], p[1], leave.at[n]) for n, p in enumerate(pairs)]
    for c in inward:
        c.start()
    for n in range(4):
        inward[n].wait()
        outward[n].start()
    for c in outward:
        c.wait()


def on_device(query_rows, key_rows, value_rows, scale_index, norm_gain, cotangent):
    full = jax.ShapeDtypeStruct((FINE + CO, COLS), BF16)
    whole = pl.BlockSpec(memory_space=pltpu.VMEM)
    scratch = [
        pltpu.VMEM((RIM, COLS), BF16),
        pltpu.VMEM((RIM, COLS), BF16),
        pltpu.VMEM((64, 16, COLS), BF16),
        pltpu.VMEM((COARSE, COLS), BF16),
        pltpu.VMEM((COARSE, COLS), BF16),
        pltpu.VMEM((3, SPAN, BLOCK), F32),
        pltpu.VMEM((SLOTS, COARSE), F32),
        pltpu.VMEM((HEADS, HEAD_DIM, FINE), F32),
        pltpu.VMEM((HEADS, HEAD_DIM, FINE), BF16),
        pltpu.VMEM((HEADS, HEAD_DIM, FINE), BF16),
        pltpu.VMEM((HEADS, 1, FINE), F32),
        pltpu.VMEM((HEADS, 1, FINE), F32),
        pltpu.VMEM((HEADS, HEAD_DIM, FINE), F32),
        pltpu.VMEM((16, FINE), F32),
        pltpu.VMEM((3, 16, FINE), F32),
        pltpu.VMEM((2, CO, COLS), F32),
        pltpu.VMEM((SLOTS, COLS), BF16),
        pltpu.VMEM((SLOTS, COLS), BF16),
        pltpu.VMEM((COARSE, COLS), F32),
        pltpu.VMEM((COARSE, COLS), F32),
        pltpu.VMEM((HEADS, 1, FINE), F32),
        pltpu.VMEM((HEADS, 1, FINE), F32),
        pltpu.VMEM((HEADS, HEAD_DIM, FINE), F32),
        pltpu.VMEM((HEADS, FINE, HEAD_DIM), F32),
        pltpu.VMEM((HEADS, FINE, HEAD_DIM), F32),
        pltpu.VMEM((2, BLOCK, COLS), BF16),
        pltpu.VMEM((2, BLOCK, COLS), BF16),
        pltpu.VMEM((4, BLOCK, COLS), BF16),
        pltpu.VMEM((4, BLOCK, COLS), BF16),
        pltpu.VMEM((3, 2, 32, COLS), BF16),
        pltpu.VMEM((3, 2, 32, COLS), BF16),
        pltpu.VMEM((3, 2 * CO, COLS), BF16),
        pltpu.VMEM((3, 2 * CO, COLS), BF16),
        pltpu.VMEM((2, HEADS, 2, WIN, HEAD_DIM), BF16),
        pltpu.VMEM((2, HEADS, 2, WIN, HEAD_DIM), BF16),
        pltpu.VMEM((CHUNKS, CHUNK, COLS), BF16),
        pltpu.VMEM((HEADS, WIN, HEAD_DIM), BF16),
        pltpu.SemaphoreType.DMA((COPIES,)),
        pltpu.SemaphoreType.DMA((COPIES,)),
    ]
    results = pl.pallas_call(
        kernel,
        out_shape=[full] * 4,
        in_specs=[whole] * 6,
        out_specs=[whole] * 4,
        scratch_shapes=scratch,
        compiler_params=pltpu.CompilerParams(
            collective_id=0, has_side_effects=True, vmem_limit_bytes=56 * 1024 * 1024
        ),
    )(query_rows, key_rows, value_rows, cotangent, norm_gain, scale_index)
    anywhere = pl.BlockSpec(memory_space=pl.ANY)
    return tuple(pl.pallas_call(
        deliver,
        out_shape=[full] * 4,
        in_specs=[anywhere] * 4,
        out_specs=[anywhere] * 4,
        scratch_shapes=[
            pltpu.VMEM((4, FINE + CO, COLS), BF16),
            pltpu.SemaphoreType.DMA((4,)),
            pltpu.SemaphoreType.DMA((4,)),
        ],
    )(*results))


def solution(mesh):
    both = P("space", "scale")
    return jax.shard_map(
        on_device, mesh=mesh, in_specs=(both, both, both, P(), P("scale"), both),
        out_specs=(both, both, both, both), check_vma=False,
    )
```

```python
import jax
import jax.numpy as jnp
from jax import lax
from jax.experimental import pallas as pl
from jax.experimental.pallas import tpu as pltpu
from jax.sharding import PartitionSpec as P

HEAD_DIM = 128
HEADS = 7
COLS = HEADS * HEAD_DIM
D = 3584
FINE = 384
WIN = 192
RIM = FINE + 2 * WIN
CO = 8
COARSE = 512
LEVELS = 6
SLOTS = 128
BLOCK = 128
SPAN = 512
OWN = ((192, 512), (192, 576), (256, 576))
HALO = (((0, 192),), ((128, 192), (576, 640)), ((576, 768),))
NEG = -1e30
SCALING = HEAD_DIM ** (-0.5)
LOG2E = 1.4426950408889634
LN2 = 0.6931471805599453
F32 = jnp.float32
BF16 = jnp.bfloat16
MESH = pl.DeviceIdType.MESH

CHUNKS = 4
CHUNK = WIN // CHUNKS
HALF = WIN // 2
EARLY = (0, 1)
HALO_K = 0
HALO_V = HALO_K + 4
HOP = HALO_V + 2 * CHUNKS
AG_Z = HOP + 2 * CHUNKS
AG_Y = AG_Z + 3
AG_X = AG_Y + 3
AG_F = AG_X + 8
STAT = AG_F + 4
RS_OPP = STAT + 3
RS_X = RS_OPP + 2
RS_Y = RS_X + 4
RS_Z = RS_Y + 3
BACK_K = RS_Z + 3
BACK_V = BACK_K + 2 * HEADS
BACK_HOP = BACK_V + 2 * HEADS
COPIES = BACK_HOP + 2 * HEADS


def nt(a, b):
    return lax.dot_general(a, b, (((1,), (1,)), ((), ())), preferred_element_type=F32)


def nn(a, b):
    return lax.dot_general(a, b, (((1,), (0,)), ((), ())), preferred_element_type=F32)


def tn(a, b):
    return lax.dot_general(a, b, (((0,), (0,)), ((), ())), preferred_element_type=F32)


def every_head(body, carry=0, first=0, last=HEADS):
    for h in range(first, last):
        carry = body(h, carry)
    return carry


def head_cols(h):
    if isinstance(h, int):
        return slice(h * HEAD_DIM, (h + 1) * HEAD_DIM)
    return pl.ds(pl.multiple_of(h * HEAD_DIM, HEAD_DIM), HEAD_DIM)


def diagonal(rows):
    slot = lax.broadcasted_iota(jnp.int32, (rows, COLS), 0) // CO
    column = lax.broadcasted_iota(jnp.int32, (rows, COLS), 1) // HEAD_DIM
    return slot == column


def spread(piece):
    return jnp.where(diagonal(SLOTS), jnp.concatenate([piece] * (SLOTS // CO), axis=0), 0.0)


def collect(wide):
    kept = jnp.where(diagonal(SLOTS), wide, 0.0)
    total = kept[0:CO]
    for g in range(1, HEADS):
        total = total + kept[g * CO : (g + 1) * CO]
    return total


def kernel(
    q, k, v, cot, gain_ref, levels,
    of_n, of_q, of_k, of_v,
    krim, vrim, cbuf, kc, vc, masks, lmask, gt, ot, dot, logs, deltas, dqt,
    stat, stat_in, coarse_row, qd, dod, gk, gv, peaks, totals, summed, own_k, own_v,
    opp_out, opp_in, x_out, x_in, y_out, y_in, z_out, z_in, back_out, back_in,
    relay, back_relay, send, recv,
):
    t = lax.axis_index("space")
    s = lax.axis_index("scale")
    x, z, y = t // 16, (t // 4) % 4, t % 4

    def at(xx, zz, yy):
        return {"space": xx * 16 + zz * 4 + yy}

    right = {"space": (t + 1) % 64}
    left = {"space": (t + 63) % 64}
    xr, xl = at((x + 1) % 4, z, y), at((x + 3) % 4, z, y)
    ys = [at(x, z, (y + d) % 4) for d in (1, 2, 3)]
    zs = [at(x, (z + d) % 4, y) for d in (1, 2, 3)]
    ss = [{"scale": (s + d) % 4} for d in (1, 2, 3)]
    carry = [at((x + 1) % 4, (z + 1) % 4, y), at((x + 3) % 4, (z + 3) % 4, y)]

    edges = (y == 3, y == 0)
    relaying = (y == 0, y == 3)
    beside = (right, left)
    first_hop = (at(x, z, 0), at(x, z, 3))
    last_hop = (
        at((x + jnp.where(z == 3, 1, 0)) % 4, (z + 1) % 4, 0),
        at((x + jnp.where(z == 0, 3, 0)) % 4, (z + 3) % 4, 3),
    )

    def copy(src, dst, number, peer, out_number=None):
        return pltpu.make_async_remote_copy(
            src_ref=src, dst_ref=dst,
            send_sem=send.at[number if out_number is None else out_number],
            recv_sem=recv.at[number], device_id=peer, device_id_type=MESH,
        )

    pending = []

    def start(src, dst, number, peer):
        c = copy(src, dst, number, peer)
        c.start()
        pending.append(c)

    def depart_edge(side, number, hop, src, via, dst):
        @pl.when(edges[side])
        def _():
            copy(src, via, hop, first_hop[side]).start()

    def depart_inner(side, number, hop, src, via, dst):
        @pl.when(jnp.logical_not(edges[side]))
        def _():
            copy(src, dst, number, beside[side]).start()

    def depart(*transfer):
        depart_edge(*transfer)
        depart_inner(*transfer)

    def pass_on(side, number, hop, via, dst):
        @pl.when(relaying[side])
        def _():
            copy(via, via, hop, first_hop[side]).wait_recv()
            copy(via, dst, number, last_hop[side], hop).start()

    def departed(side, number, hop, src):
        @pl.when(edges[side] | relaying[side])
        def _():
            copy(src, src, hop, beside[side]).wait_send()

        @pl.when(jnp.logical_not(edges[side]))
        def _():
            copy(src, src, number, beside[side]).wait_send()

    barrier = pltpu.get_barrier_semaphore()
    greeted = [left, right, xl, xr] + ys + zs + ss + carry
    for peer in greeted:
        pl.semaphore_signal(barrier, inc=1, device_id=peer, device_id_type=MESH)

    def tail(ref):
        return ref[...].astype(F32)[FINE:]

    gain = gain_ref[...].reshape(1, COLS)
    mine = x * 16 + y * 4 + z
    cbuf[mine] = jnp.concatenate([tail(k), tail(v)], axis=0).astype(BF16)
    pl.semaphore_wait(barrier, len(greeted))

    for d in (1, 2, 3):
        start(cbuf.at[mine], cbuf.at[mine], AG_Z + d - 1, zs[d - 1])

    def chunk(side, c):
        a = c * CHUNK + (WIN if side == 0 else 0)
        b = c * CHUNK + (0 if side == 0 else WIN + FINE)
        return (
            HALO_V + side * CHUNKS + c, HOP + side * CHUNKS + c,
            v.at[a : a + CHUNK], relay.at[c], vrim.at[b : b + CHUNK],
        )

    for c in EARLY:
        for side in range(2):
            depart_edge(side, *chunk(side, c))
    halves = (
        (k, krim, slice(WIN, WIN + HALF), slice(0, HALF), right),
        (k, krim, slice(0, HALF), slice(WIN + FINE, WIN + FINE + HALF), left),
        (k, krim, slice(WIN + HALF, 2 * WIN), slice(HALF, WIN), right),
        (k, krim, slice(HALF, WIN), slice(WIN + FINE + HALF, RIM), left),
    )

    def send_keys(n, when):
        src, dst, a, b, peer = halves[n]

        @pl.when(when)
        def _():
            copy(src.at[a], dst.at[b], HALO_K + n, peer).start()

    def pass_chunk(c):
        for side in range(2):
            number, hop, _, via, dst = chunk(side, c)
            pass_on(side, number, hop, via, dst)

    def line(xx, yy):
        return cbuf.at[pl.ds(xx * 16 + yy * 4, 4)]

    krim[WIN : WIN + FINE] = k[0:FINE]
    vrim[WIN : WIN + FINE] = v[0:FINE]
    row = lax.broadcasted_iota(jnp.int32, (SPAN, BLOCK), 0)
    column = lax.broadcasted_iota(jnp.int32, (SPAN, BLOCK), 1)
    for b in range(3):
        near = (row >= column) & (row - column <= 2 * WIN)
        place = row + b * BLOCK
        here = ((place >= WIN) | (t > 0)) & ((place < WIN + FINE) | (t < 63))
        masks[b] = jnp.where(near & here, 0.0, NEG)

    nothing = jnp.zeros((1, BLOCK), F32)

    def masked(b, first, last):
        return masks[b, first - b * BLOCK : last - b * BLOCK]

    def own_keys(h, _):
        cols = head_cols(h)
        for b in range(3):
            rows = slice(b * BLOCK, (b + 1) * BLOCK)
            first, last = OWN[b]
            scores = nt(krim[first:last, cols], q[rows, cols]) * (SCALING * LOG2E)
            scores = scores + masked(b, first, last)
            peak = jnp.max(scores, axis=0, keepdims=True)
            weights = jnp.exp2(scores - peak)
            peaks[h, :, rows] = peak
            totals[h, :, rows] = jnp.sum(weights, axis=0, keepdims=True)
            summed[h, :, rows] = tn(vrim[first:last, cols], weights.astype(BF16))
        return 0

    every_head(own_keys, 0, 0, 2)
    for d in (1, 3, 2):
        got = cbuf.at[x * 16 + y * 4 + (z + 4 - d) % 4]
        copy(got, got, AG_Z + d - 1, zs[d - 1]).wait_recv()
    block = line(x, y)
    for d in (1, 3, 2):
        start(block, block, AG_Y + d - 1, ys[d - 1])
    start(block, block, AG_X + 0, xr)
    start(block, block, AG_X + 4, xl)
    pass_chunk(0)
    pass_chunk(1)
    every_head(own_keys, 0, 2, 4)

    level = jnp.broadcast_to(levels[...].astype(F32).reshape(1, COARSE), (CO, COARSE))
    lane = lax.broadcasted_iota(jnp.int32, (CO, COARSE), 1)
    asked = lane == t * CO + lax.broadcasted_iota(jnp.int32, (CO, COARSE), 0)
    own_level = jnp.sum(jnp.where(asked, level, 0.0), axis=1, keepdims=True)
    seen = jnp.sum(jnp.where(level <= own_level, 1.0, 0.0), axis=1, keepdims=True)
    lane = lax.broadcasted_iota(jnp.int32, (SLOTS, COARSE), 1)
    order = (lane // 128) * 128 + ((lane // 8) % 4) * 32 + ((lane // 32) % 4) * 8 + lane % 8
    allowed = order.astype(F32) < jnp.concatenate([seen] * (SLOTS // CO), axis=0)
    lmask[...] = jnp.where(allowed, 0.0, NEG)

    def prepare(h, _):
        cols = head_cols(h)
        gained = cot[0:FINE, cols].astype(F32) * gain_ref[cols].reshape(1, HEAD_DIM)
        for b in range(3):
            gt[h, :, b * BLOCK : (b + 1) * BLOCK] = gained[b * BLOCK : (b + 1) * BLOCK].T
        return 0

    for d in (1, 3, 2):
        block = line(x, (y + 4 - d) % 4)
        copy(block, block, AG_Y + d - 1, ys[d - 1]).wait_recv()
        start(block, block, AG_X + d, xr)
        start(block, block, AG_X + 4 + d, xl)
    for c in range(CHUNKS):
        for side in range(2):
            if c in EARLY:
                depart_inner(side, *chunk(side, c))
            else:
                depart(side, *chunk(side, c))
    for n in range(4):
        send_keys(n, y >= 0)
    every_head(own_keys, 0, 4, HEADS)
    every_head(prepare, 0, 0, HEADS)
    qd[...] = spread(tail(q)).astype(BF16)

    for d in (0, 1, 3, 2):
        yy = (y + 4 - d) % 4
        from_left, from_right = line((x + 3) % 4, yy), line((x + 1) % 4, yy)
        copy(from_left, from_left, AG_X + d, xr).wait_recv()
        if d in (0, 2):
            start(from_left, from_left, AG_F + d, xr)
        copy(from_right, from_right, AG_X + 4 + d, xl).wait_recv()
        if d in (1, 3):
            start(from_right, from_right, AG_F + d, xl)
        if d in (0, 1):
            pass_chunk(2 + d)
    for d in (0, 1, 3, 2):
        far = line((x + 2) % 4, (y + 4 - d) % 4)
        copy(far, far, AG_F + d, xr if d in (0, 2) else xl).wait_recv()

    def coarse_keys(h, _):
        cols = head_cols(h)
        both = cbuf[:, :, cols].astype(F32)
        keys = both[:, 0:CO].reshape(COARSE, HEAD_DIM).astype(BF16)
        values = both[:, CO:].reshape(COARSE, HEAD_DIM).astype(BF16)
        kc[:, cols] = keys
        vc[:, cols] = values
        for b in range(3):
            rows = slice(b * BLOCK, (b + 1) * BLOCK)
            scores = nt(keys, q[rows, cols]) * (SCALING * LOG2E)
            before = peaks[h, :, rows]
            peak = jnp.maximum(before, jnp.max(scores, axis=0, keepdims=True))
            weights = jnp.exp2(scores - peak)
            scale = jnp.exp2(before - peak)
            peaks[h, :, rows] = peak
            totals[h, :, rows] = totals[h, :, rows] * scale + jnp.sum(weights, axis=0, keepdims=True)
            summed[h, :, rows] = summed[h, :, rows] * scale + tn(values, weights.astype(BF16))
        return 0

    every_head(coarse_keys, 0, 0, HEADS)

    scores = nt(qd[...], kc[...]) * (SCALING * LOG2E) + lmask[...]
    peak = jnp.max(scores, axis=1, keepdims=True)
    weights = jnp.exp2(scores - peak)
    total = jnp.sum(weights, axis=1, keepdims=True)
    wide = nn(weights.astype(BF16), vc[...]) / total
    log_c = peak + jnp.log2(total)
    attended_c = collect(wide).astype(BF16).astype(F32)
    gained_c = tail(cot) * gain
    squares_c = jnp.sum(attended_c * attended_c, axis=1, keepdims=True)
    crossed_c = jnp.sum(attended_c * gained_c, axis=1, keepdims=True)

    for n, (src, dst, a, b, peer) in enumerate(halves):
        copy(src.at[a], dst.at[b], HALO_K + n, peer).wait()
    for c in range(CHUNKS):
        for side in range(2):
            number, _, _, _, dst = chunk(side, c)
            copy(dst, dst, number, beside[side]).wait_recv()

    def halo_keys(h, sums):
        cols = head_cols(h)
        out = []
        for b in range(3):
            rows = slice(b * BLOCK, (b + 1) * BLOCK)
            peak = before = peaks[h, :, rows]
            scores = []
            for first, last in HALO[b]:
                part = nt(krim[first:last, cols], q[rows, cols]) * (SCALING * LOG2E)
                part = part + masked(b, first, last)
                scores.append(part)
                peak = jnp.maximum(peak, jnp.max(part, axis=0, keepdims=True))
            scale = jnp.exp2(before - peak)
            total, total_out = totals[h, :, rows] * scale, summed[h, :, rows] * scale
            for (first, last), part in zip(HALO[b], scores):
                weights = jnp.exp2(part - peak)
                total = total + jnp.sum(weights, axis=0, keepdims=True)
                total_out = total_out + tn(vrim[first:last, cols], weights.astype(BF16))
            attended = (total_out / total).astype(BF16)
            ot[h, :, rows] = attended
            logs[h, :, rows] = peak + jnp.log2(total)
            attended = attended.astype(F32)
            squares, crossed = sums[b]
            out.append((
                squares + jnp.sum(attended * attended, axis=0, keepdims=True),
                crossed + jnp.sum(attended * gt[h, :, rows], axis=0, keepdims=True),
            ))
        return tuple(out)

    sums = every_head(halo_keys, ((nothing, nothing),) * 3, 0, HEADS)

    stat[...] = jnp.zeros_like(stat)
    for b in range(3):
        stat[0:1, b * BLOCK : (b + 1) * BLOCK] = sums[b][0]
        stat[1:2, b * BLOCK : (b + 1) * BLOCK] = sums[b][1]
    stat[8:16, 0:BLOCK] = jnp.broadcast_to(squares_c, (CO, BLOCK))
    stat[8:16, BLOCK : 2 * BLOCK] = jnp.broadcast_to(crossed_c, (CO, BLOCK))
    for d in (1, 2, 3):
        start(stat, stat_in.at[d - 1], STAT + d - 1, ss[d - 1])
    for d in (1, 2, 3):
        copy(stat, stat_in.at[d - 1], STAT + d - 1, ss[d - 1]).wait_recv()
    whole = stat[...] + stat_in[0] + stat_in[1] + stat_in[2]
    inverse = lax.rsqrt(whole[0:1] / D + 1e-06)
    factor = inverse * inverse * inverse * (whole[1:2] / D)
    inverse_c = lax.rsqrt(whole[8:16, 0:1] / D + 1e-06)
    factor_c = inverse_c * inverse_c * inverse_c * (whole[8:16, BLOCK : BLOCK + 1] / D)

    normed_c = attended_c * inverse_c * gain
    grad_c = (inverse_c * gained_c - attended_c * factor_c).astype(BF16).astype(F32)
    grad_d = spread(grad_c)
    dod[...] = grad_d.astype(BF16)
    delta_c = jnp.sum(grad_d * spread(attended_c), axis=1, keepdims=True)

    def turn(h, _):
        attended = ot[h].astype(F32)
        grad = (inverse * gt[h] - attended * factor).astype(BF16)
        dot[h] = grad
        deltas[h] = jnp.sum(grad.astype(F32) * attended, axis=0, keepdims=True)
        return 0

    every_head(turn, 0, 0, HEADS)

    def back(side, h):
        return (
            BACK_V + side * HEADS + h, BACK_HOP + side * HEADS + h,
            back_out.at[side, h, 1], back_relay.at[h], back_in.at[side, h, 1],
        )

    def gradients(h, b, first, last):
        cols = head_cols(h)
        rows = slice(b * BLOCK, (b + 1) * BLOCK)
        keys, values = krim[first:last, cols], vrim[first:last, cols]
        queries, grads = q[rows, cols], dot[h, :, rows]
        scores = nt(keys, queries) * (SCALING * LOG2E) + masked(b, first, last)
        probs = jnp.exp2(scores - logs[h, :, rows])
        grad_probs = nn(values, grads)
        grad_scores = (probs * (grad_probs - deltas[h, :, rows])).astype(BF16)
        return (
            tn(keys, grad_scores), nn(grad_scores, queries) * SCALING, nt(probs.astype(BF16), grads)
        )

    def halo_grads(h, _):
        q0, k0, v0 = gradients(h, 0, 0, 192)
        q1, k1, v1 = gradients(h, 1, 128, 192)
        q2, k2, v2 = gradients(h, 1, 576, 640)
        q3, k3, v3 = gradients(h, 2, 576, 768)
        dqt[h] = dqt[h] + jnp.concatenate([q0, q1 + q2, q3], axis=1)
        for n, (a, b, c, d) in enumerate(((k0, k1, k2, k3), (v0, v1, v2, v3))):
            back_out[1, h, n, 0:128] = a[0:128].astype(BF16)
            back_out[1, h, n, 128:192] = (a[128:192] + b).astype(BF16)
            back_out[0, h, n, 0:64] = (d[0:64] + c).astype(BF16)
            back_out[0, h, n, 64:192] = d[64:192].astype(BF16)
        for side in range(2):
            depart(side, *back(side, h))
            copy(
                back_out.at[side, h, 0], back_in.at[side, h, 0], BACK_K + side * HEADS + h,
                beside[side],
            ).start()
        return 0

    def pass_back(first, last):
        def body(h, _):
            for side in range(2):
                number, hop, _, via, dst = back(side, h)
                pass_on(side, number, hop, via, dst)
            return 0

        every_head(body, 0, first, last)


    scores = nt(qd[...], kc[...]) * (SCALING * LOG2E) + lmask[...]
    probs = jnp.exp2(scores - log_c)
    grad_probs = nt(dod[...], vc[...])
    grad_scores = (probs * (grad_probs - delta_c)).astype(BF16)
    query_c = collect(nn(grad_scores, kc[...])) * SCALING
    coarse_row[0] = normed_c
    coarse_row[1] = query_c
    gk[...] = tn(grad_scores, qd[...])
    gv[...] = tn(probs.astype(BF16), dod[...])

    def coarse_block(j):
        rows = pl.ds(pl.multiple_of(j * BLOCK, BLOCK), BLOCK)

        def body(h, _):
            cols = head_cols(h)
            keys, values = kc[rows, cols], vc[rows, cols]
            queries, grads = q[0:FINE, cols], dot[h]
            probs = jnp.exp2(nt(keys, queries) * (SCALING * LOG2E) - logs[h])
            grad_probs = nn(values, grads)
            grad_scores = (probs * (grad_probs - deltas[h])).astype(BF16)
            gv[rows, cols] = gv[rows, cols] + nt(probs.astype(BF16), grads)
            gk[rows, cols] = (gk[rows, cols] + nn(grad_scores, queries)) * SCALING
            part = tn(keys, grad_scores)
            dqt[h] = dqt[h] + part
            return 0

        every_head(body, 0, 0, HEADS)
        return rows

    dqt[...] = jnp.zeros_like(dqt)
    rows = coarse_block((x + 2) % 4)
    opp_out[0] = gk[rows].astype(BF16)
    opp_out[1] = gv[rows].astype(BF16)
    start(opp_out.at[0], opp_in.at[0], RS_OPP, xr)
    start(opp_out.at[1], opp_in.at[1], RS_OPP + 1, xl)
    rows_r = coarse_block((x + 1) % 4)
    copy(opp_out.at[0], opp_in.at[0], RS_OPP, xr).wait_recv()
    x_out[0] = (gk[rows_r] + opp_in[0].astype(F32)).astype(BF16)
    x_out[1] = gv[rows_r].astype(BF16)
    start(x_out.at[0], x_in.at[0], RS_X, xr)
    start(x_out.at[1], x_in.at[1], RS_X + 1, xr)
    rows_l = coarse_block((x + 3) % 4)
    copy(opp_out.at[1], opp_in.at[1], RS_OPP + 1, xl).wait_recv()
    x_out[2] = gk[rows_l].astype(BF16)
    x_out[3] = (gv[rows_l] + opp_in[1].astype(F32)).astype(BF16)
    start(x_out.at[2], x_in.at[2], RS_X + 2, xl)
    start(x_out.at[3], x_in.at[3], RS_X + 3, xl)
    every_head(halo_grads, 0, 0, HEADS)
    own = coarse_block(x)

    pass_back(0, 2)
    def own_grads(h, _):
        for b in range(3):
            first, last = OWN[b]
            part, part_k, part_v = gradients(h, b, first, last)
            rows = slice(b * BLOCK, (b + 1) * BLOCK)
            dqt[h, :, rows] = dqt[h, :, rows] + part
            here = slice(first - WIN, last - WIN)
            if b == 0:
                own_k[h, here], own_v[h, here] = part_k, part_v
                rest = slice(last - WIN, FINE)
                own_k[h, rest] = jnp.zeros((FINE + WIN - last, HEAD_DIM), F32)
                own_v[h, rest] = jnp.zeros((FINE + WIN - last, HEAD_DIM), F32)
            else:
                own_k[h, here] = own_k[h, here] + part_k
                own_v[h, here] = own_v[h, here] + part_v
        return 0

    every_head(own_grads, 0, 0, HEADS)

    pass_back(2, 4)
    for n in range(4):
        copy(x_out.at[n], x_in.at[n], RS_X + n, xr if n < 2 else xl).wait_recv()
    gk[own] = gk[own] + x_in[0].astype(F32) + x_in[2].astype(F32)
    gv[own] = gv[own] + x_in[1].astype(F32) + x_in[3].astype(F32)

    def piece(yy, zz, size):
        return pl.ds(pl.multiple_of(x * 128 + yy * 32 + zz * CO, size), size)

    for d in (1, 2, 3):
        there = piece((y + d) % 4, 0, 32)
        y_out[d - 1, 0] = gk[there].astype(BF16)
        y_out[d - 1, 1] = gv[there].astype(BF16)
        start(y_out.at[d - 1], y_in.at[d - 1], RS_Y + d - 1, ys[d - 1])

    def finish(h, _):
        cols = head_cols(h)
        own_gain = gain_ref[cols].reshape(1, HEAD_DIM)
        queries, normed = [], []
        for b in range(3):
            rows = slice(b * BLOCK, (b + 1) * BLOCK)
            queries.append((dqt[h, :, rows] * SCALING).T)
            normed.append((ot[h, :, rows].astype(F32) * inverse[:, rows]).T * own_gain)
        of_n[:, cols] = jnp.concatenate(normed + [coarse_row[0, :, cols]], axis=0).astype(BF16)
        of_q[:, cols] = jnp.concatenate(queries + [coarse_row[1, :, cols]], axis=0).astype(BF16)
        return 0


    pass_back(4, 5)
    every_head(finish, 0, 0, HEADS)
    for d in (1, 2, 3):
        copy(y_out.at[d - 1], y_in.at[d - 1], RS_Y + d - 1, ys[d - 1]).wait_recv()
    here = piece(y, 0, 32)
    for n, total in enumerate((gk, gv)):
        total[here] = (
            total[here]
            + y_in[0, n].astype(F32) + y_in[1, n].astype(F32) + y_in[2, n].astype(F32)
        )
    for d in (1, 2, 3):
        there = piece(y, (z + d) % 4, CO)
        z_out[d - 1] = jnp.concatenate([gk[there], gv[there]], axis=0).astype(BF16)
        start(z_out.at[d - 1], z_in.at[d - 1], RS_Z + d - 1, zs[d - 1])
    pass_back(5, 7)
    for d in (1, 2, 3):
        copy(z_out.at[d - 1], z_in.at[d - 1], RS_Z + d - 1, zs[d - 1]).wait_recv()
    here = piece(y, z, CO)
    arrived = z_in[0].astype(F32) + z_in[1].astype(F32) + z_in[2].astype(F32)
    coarse_row[0] = gk[here] + arrived[0:CO]
    coarse_row[1] = gv[here] + arrived[CO:]

    def fold(h, _):
        cols = head_cols(h)
        for side in range(2):
            number, hop, src, _, dst = back(side, h)
            copy(dst, dst, number, beside[side]).wait_recv()
            departed(side, number, hop, src)
            copy(
                back_out.at[side, h, 0], back_in.at[side, h, 0], BACK_K + side * HEADS + h,
                beside[side],
            ).wait()
        for n, (mine, target) in enumerate(((own_k, of_k), (own_v, of_v))):
            parts = [
                mine[h, side * WIN : (side + 1) * WIN] + back_in[side, h, n].astype(F32)
                for side in range(2)
            ]
            target[:, cols] = jnp.concatenate(
                parts + [coarse_row[n, :, cols]], axis=0
            ).astype(BF16)
        return 0

    every_head(fold, 0, 0, HEADS)
    for c in range(CHUNKS):
        for side in range(2):
            number, hop, src, _, _ = chunk(side, c)
            departed(side, number, hop, src)
    for c in pending:
        c.wait_send()


def deliver(a, b, c, d, to_a, to_b, to_c, to_d, held, arrive, leave):
    pairs = ((a, to_a), (b, to_b), (c, to_c), (d, to_d))
    inward = [pltpu.make_async_copy(p[0], held.at[n], arrive.at[n]) for n, p in enumerate(pairs)]
    outward = [pltpu.make_async_copy(held.at[n], p[1], leave.at[n]) for n, p in enumerate(pairs)]
    for c in inward:
        c.start()
    for n in range(4):
        inward[n].wait()
        outward[n].start()
    for c in outward:
        c.wait()


def on_device(query_rows, key_rows, value_rows, scale_index, norm_gain, cotangent):
    full = jax.ShapeDtypeStruct((FINE + CO, COLS), BF16)
    whole = pl.BlockSpec(memory_space=pltpu.VMEM)
    scratch = [
        pltpu.VMEM((RIM, COLS), BF16),
        pltpu.VMEM((RIM, COLS), BF16),
        pltpu.VMEM((64, 16, COLS), BF16),
        pltpu.VMEM((COARSE, COLS), BF16),
        pltpu.VMEM((COARSE, COLS), BF16),
        pltpu.VMEM((3, SPAN, BLOCK), F32),
        pltpu.VMEM((SLOTS, COARSE), F32),
        pltpu.VMEM((HEADS, HEAD_DIM, FINE), F32),
        pltpu.VMEM((HEADS, HEAD_DIM, FINE), BF16),
        pltpu.VMEM((HEADS, HEAD_DIM, FINE), BF16),
        pltpu.VMEM((HEADS, 1, FINE), F32),
        pltpu.VMEM((HEADS, 1, FINE), F32),
        pltpu.VMEM((HEADS, HEAD_DIM, FINE), F32),
        pltpu.VMEM((16, FINE), F32),
        pltpu.VMEM((3, 16, FINE), F32),
        pltpu.VMEM((2, CO, COLS), F32),
        pltpu.VMEM((SLOTS, COLS), BF16),
        pltpu.VMEM((SLOTS, COLS), BF16),
        pltpu.VMEM((COARSE, COLS), F32),
        pltpu.VMEM((COARSE, COLS), F32),
        pltpu.VMEM((HEADS, 1, FINE), F32),
        pltpu.VMEM((HEADS, 1, FINE), F32),
        pltpu.VMEM((HEADS, HEAD_DIM, FINE), F32),
        pltpu.VMEM((HEADS, FINE, HEAD_DIM), F32),
        pltpu.VMEM((HEADS, FINE, HEAD_DIM), F32),
        pltpu.VMEM((2, BLOCK, COLS), BF16),
        pltpu.VMEM((2, BLOCK, COLS), BF16),
        pltpu.VMEM((4, BLOCK, COLS), BF16),
        pltpu.VMEM((4, BLOCK, COLS), BF16),
        pltpu.VMEM((3, 2, 32, COLS), BF16),
        pltpu.VMEM((3, 2, 32, COLS), BF16),
        pltpu.VMEM((3, 2 * CO, COLS), BF16),
        pltpu.VMEM((3, 2 * CO, COLS), BF16),
        pltpu.VMEM((2, HEADS, 2, WIN, HEAD_DIM), BF16),
        pltpu.VMEM((2, HEADS, 2, WIN, HEAD_DIM), BF16),
        pltpu.VMEM((CHUNKS, CHUNK, COLS), BF16),
        pltpu.VMEM((HEADS, WIN, HEAD_DIM), BF16),
        pltpu.SemaphoreType.DMA((COPIES,)),
        pltpu.SemaphoreType.DMA((COPIES,)),
    ]
    results = pl.pallas_call(
        kernel,
        out_shape=[full] * 4,
        in_specs=[whole] * 6,
        out_specs=[whole] * 4,
        scratch_shapes=scratch,
        compiler_params=pltpu.CompilerParams(
            collective_id=0, has_side_effects=True, vmem_limit_bytes=56 * 1024 * 1024
        ),
    )(query_rows, key_rows, value_rows, cotangent, norm_gain, scale_index)
    anywhere = pl.BlockSpec(memory_space=pl.ANY)
    return tuple(pl.pallas_call(
        deliver,
        out_shape=[full] * 4,
        in_specs=[anywhere] * 4,
        out_specs=[anywhere] * 4,
        scratch_shapes=[
            pltpu.VMEM((4, FINE + CO, COLS), BF16),
            pltpu.SemaphoreType.DMA((4,)),
            pltpu.SemaphoreType.DMA((4,)),
        ],
    )(*results))


def solution(mesh):
    both = P("space", "scale")
    return jax.shard_map(
        on_device, mesh=mesh, in_specs=(both, both, both, P(), P("scale"), both),
        out_specs=(both, both, both, both), check_vma=False,
    )
```

```python
import jax
import jax.numpy as jnp
from jax import lax
from jax.experimental import pallas as pl
from jax.experimental.pallas import tpu as pltpu
from jax.sharding import PartitionSpec as P

HEAD_DIM = 128
HEADS = 7
COLS = HEADS * HEAD_DIM
D = 3584
FINE = 384
WIN = 192
RIM = FINE + 2 * WIN
CO = 8
COARSE = 512
LEVELS = 6
SLOTS = 128
BLOCK = 128
SPAN = 512
OWN = ((192, 512), (192, 576), (256, 576))
HALO = (((0, 192),), ((128, 192), (576, 640)), ((576, 768),))
NEG = -1e30
SCALING = HEAD_DIM ** (-0.5)
LOG2E = 1.4426950408889634
LN2 = 0.6931471805599453
F32 = jnp.float32
BF16 = jnp.bfloat16
MESH = pl.DeviceIdType.MESH

CHUNKS = 4
CHUNK = WIN // CHUNKS
HALF = WIN // 2
EARLY = (0, 1)
HALO_K = 0
HALO_V = HALO_K + 4
HOP = HALO_V + 2 * CHUNKS
AG_Z = HOP + 2 * CHUNKS
AG_Y = AG_Z + 3
AG_X = AG_Y + 3
AG_F = AG_X + 8
STAT = AG_F + 4
RS_OPP = STAT + 3
RS_X = RS_OPP + 2
RS_Y = RS_X + 4
RS_Z = RS_Y + 3
BACK_K = RS_Z + 3
BACK_V = BACK_K + 2 * HEADS
BACK_HOP = BACK_V + 2 * HEADS
COPIES = BACK_HOP + 2 * HEADS


def nt(a, b):
    return lax.dot_general(a, b, (((1,), (1,)), ((), ())), preferred_element_type=F32)


def nn(a, b):
    return lax.dot_general(a, b, (((1,), (0,)), ((), ())), preferred_element_type=F32)


def tn(a, b):
    return lax.dot_general(a, b, (((0,), (0,)), ((), ())), preferred_element_type=F32)


def every_head(body, carry=0, first=0, last=HEADS):
    for h in range(first, last):
        carry = body(h, carry)
    return carry


def head_cols(h):
    if isinstance(h, int):
        return slice(h * HEAD_DIM, (h + 1) * HEAD_DIM)
    return pl.ds(pl.multiple_of(h * HEAD_DIM, HEAD_DIM), HEAD_DIM)


def diagonal(rows):
    slot = lax.broadcasted_iota(jnp.int32, (rows, COLS), 0) // CO
    column = lax.broadcasted_iota(jnp.int32, (rows, COLS), 1) // HEAD_DIM
    return slot == column


def spread(piece):
    return jnp.where(diagonal(SLOTS), jnp.concatenate([piece] * (SLOTS // CO), axis=0), 0.0)


def collect(wide):
    kept = jnp.where(diagonal(SLOTS), wide, 0.0)
    total = kept[0:CO]
    for g in range(1, HEADS):
        total = total + kept[g * CO : (g + 1) * CO]
    return total


def kernel(
    q, k, v, cot, gain_ref, levels,
    of_n, of_q, of_k, of_v,
    krim, vrim, cbuf, kc, vc, masks, lmask, gt, ot, dot, logs, deltas, dqt,
    stat, stat_in, coarse_row, qd, dod, gk, gv, peaks, totals, summed, own_k, own_v,
    opp_out, opp_in, x_out, x_in, y_out, y_in, z_out, z_in, back_out, back_in,
    relay, back_relay, send, recv,
):
    t = lax.axis_index("space")
    s = lax.axis_index("scale")
    x, z, y = t // 16, (t // 4) % 4, t % 4

    def at(xx, zz, yy):
        return {"space": xx * 16 + zz * 4 + yy}

    right = {"space": (t + 1) % 64}
    left = {"space": (t + 63) % 64}
    xr, xl = at((x + 1) % 4, z, y), at((x + 3) % 4, z, y)
    ys = [at(x, z, (y + d) % 4) for d in (1, 2, 3)]
    zs = [at(x, (z + d) % 4, y) for d in (1, 2, 3)]
    ss = [{"scale": (s + d) % 4} for d in (1, 2, 3)]
    carry = [at((x + 1) % 4, (z + 1) % 4, y), at((x + 3) % 4, (z + 3) % 4, y)]

    edges = (y == 3, y == 0)
    relaying = (y == 0, y == 3)
    beside = (right, left)
    first_hop = (at(x, z, 0), at(x, z, 3))
    last_hop = (
        at((x + jnp.where(z == 3, 1, 0)) % 4, (z + 1) % 4, 0),
        at((x + jnp.where(z == 0, 3, 0)) % 4, (z + 3) % 4, 3),
    )

    def copy(src, dst, number, peer, out_number=None):
        return pltpu.make_async_remote_copy(
            src_ref=src, dst_ref=dst,
            send_sem=send.at[number if out_number is None else out_number],
            recv_sem=recv.at[number], device_id=peer, device_id_type=MESH,
        )

    pending = []

    def start(src, dst, number, peer):
        c = copy(src, dst, number, peer)
        c.start()
        pending.append(c)

    def depart_edge(side, number, hop, src, via, dst):
        @pl.when(edges[side])
        def _():
            copy(src, via, hop, first_hop[side]).start()

    def depart_inner(side, number, hop, src, via, dst):
        @pl.when(jnp.logical_not(edges[side]))
        def _():
            copy(src, dst, number, beside[side]).start()

    def depart(*transfer):
        depart_edge(*transfer)
        depart_inner(*transfer)

    def pass_on(side, number, hop, via, dst):
        @pl.when(relaying[side])
        def _():
            copy(via, via, hop, first_hop[side]).wait_recv()
            copy(via, dst, number, last_hop[side], hop).start()

    def departed(side, number, hop, src):
        @pl.when(edges[side] | relaying[side])
        def _():
            copy(src, src, hop, beside[side]).wait_send()

        @pl.when(jnp.logical_not(edges[side]))
        def _():
            copy(src, src, number, beside[side]).wait_send()

    barrier = pltpu.get_barrier_semaphore()
    greeted = [left, right, xl, xr] + ys + zs + ss + carry
    for peer in greeted:
        pl.semaphore_signal(barrier, inc=1, device_id=peer, device_id_type=MESH)

    def tail(ref):
        return ref[...].astype(F32)[FINE:]

    gain = gain_ref[...].reshape(1, COLS)
    mine = x * 16 + y * 4 + z
    cbuf[mine] = jnp.concatenate([tail(k), tail(v)], axis=0).astype(BF16)
    pl.semaphore_wait(barrier, len(greeted))

    for d in (1, 2, 3):
        start(cbuf.at[mine], cbuf.at[mine], AG_Z + d - 1, zs[d - 1])

    def chunk(side, c):
        a = c * CHUNK + (WIN if side == 0 else 0)
        b = c * CHUNK + (0 if side == 0 else WIN + FINE)
        return (
            HALO_V + side * CHUNKS + c, HOP + side * CHUNKS + c,
            v.at[a : a + CHUNK], relay.at[c], vrim.at[b : b + CHUNK],
        )

    for c in EARLY:
        for side in range(2):
            depart_edge(side, *chunk(side, c))
    halves = (
        (k, krim, slice(WIN, WIN + HALF), slice(0, HALF), right),
        (k, krim, slice(0, HALF), slice(WIN + FINE, WIN + FINE + HALF), left),
        (k, krim, slice(WIN + HALF, 2 * WIN), slice(HALF, WIN), right),
        (k, krim, slice(HALF, WIN), slice(WIN + FINE + HALF, RIM), left),
    )

    def send_keys(n, when):
        src, dst, a, b, peer = halves[n]

        @pl.when(when)
        def _():
            copy(src.at[a], dst.at[b], HALO_K + n, peer).start()

    def pass_chunk(c):
        for side in range(2):
            number, hop, _, via, dst = chunk(side, c)
            pass_on(side, number, hop, via, dst)

    def line(xx, yy):
        return cbuf.at[pl.ds(xx * 16 + yy * 4, 4)]

    krim[WIN : WIN + FINE] = k[0:FINE]
    vrim[WIN : WIN + FINE] = v[0:FINE]
    row = lax.broadcasted_iota(jnp.int32, (SPAN, BLOCK), 0)
    column = lax.broadcasted_iota(jnp.int32, (SPAN, BLOCK), 1)
    for b in range(3):
        near = (row >= column) & (row - column <= 2 * WIN)
        place = row + b * BLOCK
        here = ((place >= WIN) | (t > 0)) & ((place < WIN + FINE) | (t < 63))
        masks[b] = jnp.where(near & here, 0.0, NEG)

    nothing = jnp.zeros((1, BLOCK), F32)

    def masked(b, first, last):
        return masks[b, first - b * BLOCK : last - b * BLOCK]

    def own_keys(h, _):
        cols = head_cols(h)
        for b in range(3):
            rows = slice(b * BLOCK, (b + 1) * BLOCK)
            first, last = OWN[b]
            scores = nt(krim[first:last, cols], q[rows, cols]) * (SCALING * LOG2E)
            scores = scores + masked(b, first, last)
            peak = jnp.max(scores, axis=0, keepdims=True)
            weights = jnp.exp2(scores - peak)
            peaks[h, :, rows] = peak
            totals[h, :, rows] = jnp.sum(weights, axis=0, keepdims=True)
            summed[h, :, rows] = tn(vrim[first:last, cols], weights.astype(BF16))
        return 0

    every_head(own_keys, 0, 0, 2)
    for d in (1, 3, 2):
        got = cbuf.at[x * 16 + y * 4 + (z + 4 - d) % 4]
        copy(got, got, AG_Z + d - 1, zs[d - 1]).wait_recv()
    block = line(x, y)
    for d in (1, 3, 2):
        start(block, block, AG_Y + d - 1, ys[d - 1])
    start(block, block, AG_X + 0, xr)
    start(block, block, AG_X + 4, xl)
    pass_chunk(0)
    pass_chunk(1)
    every_head(own_keys, 0, 2, 4)

    level = jnp.broadcast_to(levels[...].astype(F32).reshape(1, COARSE), (CO, COARSE))
    lane = lax.broadcasted_iota(jnp.int32, (CO, COARSE), 1)
    asked = lane == t * CO + lax.broadcasted_iota(jnp.int32, (CO, COARSE), 0)
    own_level = jnp.sum(jnp.where(asked, level, 0.0), axis=1, keepdims=True)
    seen = jnp.sum(jnp.where(level <= own_level, 1.0, 0.0), axis=1, keepdims=True)
    lane = lax.broadcasted_iota(jnp.int32, (SLOTS, COARSE), 1)
    order = (lane // 128) * 128 + ((lane // 8) % 4) * 32 + ((lane // 32) % 4) * 8 + lane % 8
    allowed = order.astype(F32) < jnp.concatenate([seen] * (SLOTS // CO), axis=0)
    lmask[...] = jnp.where(allowed, 0.0, NEG)

    def prepare(h, _):
        cols = head_cols(h)
        gained = cot[0:FINE, cols].astype(F32) * gain_ref[cols].reshape(1, HEAD_DIM)
        for b in range(3):
            gt[h, :, b * BLOCK : (b + 1) * BLOCK] = gained[b * BLOCK : (b + 1) * BLOCK].T
        return 0

    for d in (1, 3, 2):
        block = line(x, (y + 4 - d) % 4)
        copy(block, block, AG_Y + d - 1, ys[d - 1]).wait_recv()
        start(block, block, AG_X + d, xr)
        start(block, block, AG_X + 4 + d, xl)
    for c in range(CHUNKS):
        for side in range(2):
            if c in EARLY:
                depart_inner(side, *chunk(side, c))
            else:
                depart(side, *chunk(side, c))
    for n in range(4):
        send_keys(n, y >= 0)
    every_head(own_keys, 0, 4, HEADS)
    every_head(prepare, 0, 0, HEADS)
    qd[...] = spread(tail(q)).astype(BF16)

    for d in (0, 1, 3, 2):
        yy = (y + 4 - d) % 4
        from_left, from_right = line((x + 3) % 4, yy), line((x + 1) % 4, yy)
        copy(from_left, from_left, AG_X + d, xr).wait_recv()
        if d in (0, 2):
            start(from_left, from_left, AG_F + d, xr)
        copy(from_right, from_right, AG_X + 4 + d, xl).wait_recv()
        if d in (1, 3):
            start(from_right, from_right, AG_F + d, xl)
        if d in (0, 1):
            pass_chunk(2 + d)
    for d in (0, 1, 3, 2):
        far = line((x + 2) % 4, (y + 4 - d) % 4)
        copy(far, far, AG_F + d, xr if d in (0, 2) else xl).wait_recv()

    def coarse_keys(h, _):
        cols = head_cols(h)
        both = cbuf[:, :, cols].astype(F32)
        keys = both[:, 0:CO].reshape(COARSE, HEAD_DIM).astype(BF16)
        values = both[:, CO:].reshape(COARSE, HEAD_DIM).astype(BF16)
        kc[:, cols] = keys
        vc[:, cols] = values
        for b in range(3):
            rows = slice(b * BLOCK, (b + 1) * BLOCK)
            scores = nt(keys, q[rows, cols]) * (SCALING * LOG2E)
            before = peaks[h, :, rows]
            peak = jnp.maximum(before, jnp.max(scores, axis=0, keepdims=True))
            weights = jnp.exp2(scores - peak)
            scale = jnp.exp2(before - peak)
            peaks[h, :, rows] = peak
            totals[h, :, rows] = totals[h, :, rows] * scale + jnp.sum(weights, axis=0, keepdims=True)
            summed[h, :, rows] = summed[h, :, rows] * scale + tn(values, weights.astype(BF16))
        return 0

    every_head(coarse_keys, 0, 0, HEADS)

    scores = nt(qd[...], kc[...]) * (SCALING * LOG2E) + lmask[...]
    peak = jnp.max(scores, axis=1, keepdims=True)
    weights = jnp.exp2(scores - peak)
    total = jnp.sum(weights, axis=1, keepdims=True)
    wide = nn(weights.astype(BF16), vc[...]) / total
    log_c = peak + jnp.log2(total)
    probs = jnp.exp2(scores - log_c)
    attended_c = collect(wide).astype(BF16).astype(F32)
    gained_c = tail(cot) * gain
    squares_c = jnp.sum(attended_c * attended_c, axis=1, keepdims=True)
    crossed_c = jnp.sum(attended_c * gained_c, axis=1, keepdims=True)

    for n, (src, dst, a, b, peer) in enumerate(halves):
        copy(src.at[a], dst.at[b], HALO_K + n, peer).wait()
    for c in range(CHUNKS):
        for side in range(2):
            number, _, _, _, dst = chunk(side, c)
            copy(dst, dst, number, beside[side]).wait_recv()

    def halo_keys(h, sums):
        cols = head_cols(h)
        out = []
        for b in range(3):
            rows = slice(b * BLOCK, (b + 1) * BLOCK)
            peak = before = peaks[h, :, rows]
            scores = []
            for first, last in HALO[b]:
                part = nt(krim[first:last, cols], q[rows, cols]) * (SCALING * LOG2E)
                part = part + masked(b, first, last)
                scores.append(part)
                peak = jnp.maximum(peak, jnp.max(part, axis=0, keepdims=True))
            scale = jnp.exp2(before - peak)
            total, total_out = totals[h, :, rows] * scale, summed[h, :, rows] * scale
            for (first, last), part in zip(HALO[b], scores):
                weights = jnp.exp2(part - peak)
                total = total + jnp.sum(weights, axis=0, keepdims=True)
                total_out = total_out + tn(vrim[first:last, cols], weights.astype(BF16))
            attended = (total_out / total).astype(BF16)
            ot[h, :, rows] = attended
            logs[h, :, rows] = peak + jnp.log2(total)
            attended = attended.astype(F32)
            squares, crossed = sums[b]
            out.append((
                squares + jnp.sum(attended * attended, axis=0, keepdims=True),
                crossed + jnp.sum(attended * gt[h, :, rows], axis=0, keepdims=True),
            ))
        return tuple(out)

    sums = every_head(halo_keys, ((nothing, nothing),) * 3, 0, HEADS)

    stat[...] = jnp.zeros_like(stat)
    for b in range(3):
        stat[0:1, b * BLOCK : (b + 1) * BLOCK] = sums[b][0]
        stat[1:2, b * BLOCK : (b + 1) * BLOCK] = sums[b][1]
    stat[8:16, 0:BLOCK] = jnp.broadcast_to(squares_c, (CO, BLOCK))
    stat[8:16, BLOCK : 2 * BLOCK] = jnp.broadcast_to(crossed_c, (CO, BLOCK))
    for d in (1, 2, 3):
        start(stat, stat_in.at[d - 1], STAT + d - 1, ss[d - 1])
    for d in (1, 2, 3):
        copy(stat, stat_in.at[d - 1], STAT + d - 1, ss[d - 1]).wait_recv()
    whole = stat[...] + stat_in[0] + stat_in[1] + stat_in[2]
    inverse = lax.rsqrt(whole[0:1] / D + 1e-06)
    factor = inverse * inverse * inverse * (whole[1:2] / D)
    inverse_c = lax.rsqrt(whole[8:16, 0:1] / D + 1e-06)
    factor_c = inverse_c * inverse_c * inverse_c * (whole[8:16, BLOCK : BLOCK + 1] / D)

    normed_c = attended_c * inverse_c * gain
    grad_c = (inverse_c * gained_c - attended_c * factor_c).astype(BF16).astype(F32)
    grad_d = spread(grad_c)
    dod[...] = grad_d.astype(BF16)
    delta_c = jnp.sum(grad_d * spread(attended_c), axis=1, keepdims=True)

    def turn(h, _):
        attended = ot[h].astype(F32)
        grad = (inverse * gt[h] - attended * factor).astype(BF16)
        dot[h] = grad
        deltas[h] = jnp.sum(grad.astype(F32) * attended, axis=0, keepdims=True)
        return 0

    every_head(turn, 0, 0, HEADS)

    def back(side, h):
        return (
            BACK_V + side * HEADS + h, BACK_HOP + side * HEADS + h,
            back_out.at[side, h, 1], back_relay.at[h], back_in.at[side, h, 1],
        )

    def gradients(h, b, first, last):
        cols = head_cols(h)
        rows = slice(b * BLOCK, (b + 1) * BLOCK)
        keys, values = krim[first:last, cols], vrim[first:last, cols]
        queries, grads = q[rows, cols], dot[h, :, rows]
        scores = nt(keys, queries) * (SCALING * LOG2E) + masked(b, first, last)
        probs = jnp.exp2(scores - logs[h, :, rows])
        grad_probs = nn(values, grads)
        grad_scores = (probs * (grad_probs - deltas[h, :, rows])).astype(BF16)
        return (
            tn(keys, grad_scores), nn(grad_scores, queries) * SCALING, nt(probs.astype(BF16), grads)
        )

    def halo_grads(h, _):
        q0, k0, v0 = gradients(h, 0, 0, 192)
        q1, k1, v1 = gradients(h, 1, 128, 192)
        q2, k2, v2 = gradients(h, 1, 576, 640)
        q3, k3, v3 = gradients(h, 2, 576, 768)
        dqt[h] = dqt[h] + jnp.concatenate([q0, q1 + q2, q3], axis=1)
        for n, (a, b, c, d) in enumerate(((k0, k1, k2, k3), (v0, v1, v2, v3))):
            back_out[1, h, n, 0:128] = a[0:128].astype(BF16)
            back_out[1, h, n, 128:192] = (a[128:192] + b).astype(BF16)
            back_out[0, h, n, 0:64] = (d[0:64] + c).astype(BF16)
            back_out[0, h, n, 64:192] = d[64:192].astype(BF16)
        for side in range(2):
            depart(side, *back(side, h))
            copy(
                back_out.at[side, h, 0], back_in.at[side, h, 0], BACK_K + side * HEADS + h,
                beside[side],
            ).start()
        return 0

    def pass_back(first, last):
        def body(h, _):
            for side in range(2):
                number, hop, _, via, dst = back(side, h)
                pass_on(side, number, hop, via, dst)
            return 0

        every_head(body, 0, first, last)


    grad_probs = nt(dod[...], vc[...])
    grad_scores = (probs * (grad_probs - delta_c)).astype(BF16)
    query_c = collect(nn(grad_scores, kc[...])) * SCALING
    coarse_row[0] = normed_c
    coarse_row[1] = query_c
    gk[...] = tn(grad_scores, qd[...])
    gv[...] = tn(probs.astype(BF16), dod[...])

    def coarse_block(j):
        rows = pl.ds(pl.multiple_of(j * BLOCK, BLOCK), BLOCK)

        def body(h, _):
            cols = head_cols(h)
            keys, values = kc[rows, cols], vc[rows, cols]
            queries, grads = q[0:FINE, cols], dot[h]
            probs = jnp.exp2(nt(keys, queries) * (SCALING * LOG2E) - logs[h])
            grad_probs = nn(values, grads)
            grad_scores = (probs * (grad_probs - deltas[h])).astype(BF16)
            gv[rows, cols] = gv[rows, cols] + nt(probs.astype(BF16), grads)
            gk[rows, cols] = (gk[rows, cols] + nn(grad_scores, queries)) * SCALING
            part = tn(keys, grad_scores)
            dqt[h] = dqt[h] + part
            return 0

        every_head(body, 0, 0, HEADS)
        return rows

    dqt[...] = jnp.zeros_like(dqt)
    rows = coarse_block((x + 2) % 4)
    opp_out[0] = gk[rows].astype(BF16)
    opp_out[1] = gv[rows].astype(BF16)
    start(opp_out.at[0], opp_in.at[0], RS_OPP, xr)
    start(opp_out.at[1], opp_in.at[1], RS_OPP + 1, xl)
    rows_r = coarse_block((x + 1) % 4)
    copy(opp_out.at[0], opp_in.at[0], RS_OPP, xr).wait_recv()
    x_out[0] = (gk[rows_r] + opp_in[0].astype(F32)).astype(BF16)
    x_out[1] = gv[rows_r].astype(BF16)
    start(x_out.at[0], x_in.at[0], RS_X, xr)
    start(x_out.at[1], x_in.at[1], RS_X + 1, xr)
    rows_l = coarse_block((x + 3) % 4)
    copy(opp_out.at[1], opp_in.at[1], RS_OPP + 1, xl).wait_recv()
    x_out[2] = gk[rows_l].astype(BF16)
    x_out[3] = (gv[rows_l] + opp_in[1].astype(F32)).astype(BF16)
    start(x_out.at[2], x_in.at[2], RS_X + 2, xl)
    start(x_out.at[3], x_in.at[3], RS_X + 3, xl)
    every_head(halo_grads, 0, 0, HEADS)
    own = coarse_block(x)

    pass_back(0, 2)
    def own_grads(h, _):
        for b in range(3):
            first, last = OWN[b]
            part, part_k, part_v = gradients(h, b, first, last)
            rows = slice(b * BLOCK, (b + 1) * BLOCK)
            dqt[h, :, rows] = dqt[h, :, rows] + part
            here = slice(first - WIN, last - WIN)
            if b == 0:
                own_k[h, here], own_v[h, here] = part_k, part_v
                rest = slice(last - WIN, FINE)
                own_k[h, rest] = jnp.zeros((FINE + WIN - last, HEAD_DIM), F32)
                own_v[h, rest] = jnp.zeros((FINE + WIN - last, HEAD_DIM), F32)
            else:
                own_k[h, here] = own_k[h, here] + part_k
                own_v[h, here] = own_v[h, here] + part_v
        return 0

    every_head(own_grads, 0, 0, HEADS)

    pass_back(2, 4)
    for n in range(4):
        copy(x_out.at[n], x_in.at[n], RS_X + n, xr if n < 2 else xl).wait_recv()
    gk[own] = gk[own] + x_in[0].astype(F32) + x_in[2].astype(F32)
    gv[own] = gv[own] + x_in[1].astype(F32) + x_in[3].astype(F32)

    def piece(yy, zz, size):
        return pl.ds(pl.multiple_of(x * 128 + yy * 32 + zz * CO, size), size)

    for d in (1, 2, 3):
        there = piece((y + d) % 4, 0, 32)
        y_out[d - 1, 0] = gk[there].astype(BF16)
        y_out[d - 1, 1] = gv[there].astype(BF16)
        start(y_out.at[d - 1], y_in.at[d - 1], RS_Y + d - 1, ys[d - 1])

    def finish(h, _):
        cols = head_cols(h)
        own_gain = gain_ref[cols].reshape(1, HEAD_DIM)
        queries, normed = [], []
        for b in range(3):
            rows = slice(b * BLOCK, (b + 1) * BLOCK)
            queries.append((dqt[h, :, rows] * SCALING).T)
            normed.append((ot[h, :, rows].astype(F32) * inverse[:, rows]).T * own_gain)
        of_n[:, cols] = jnp.concatenate(normed + [coarse_row[0, :, cols]], axis=0).astype(BF16)
        of_q[:, cols] = jnp.concatenate(queries + [coarse_row[1, :, cols]], axis=0).astype(BF16)
        return 0


    pass_back(4, 5)
    every_head(finish, 0, 0, HEADS)
    for d in (1, 2, 3):
        copy(y_out.at[d - 1], y_in.at[d - 1], RS_Y + d - 1, ys[d - 1]).wait_recv()
    here = piece(y, 0, 32)
    for n, total in enumerate((gk, gv)):
        total[here] = (
            total[here]
            + y_in[0, n].astype(F32) + y_in[1, n].astype(F32) + y_in[2, n].astype(F32)
        )
    for d in (1, 2, 3):
        there = piece(y, (z + d) % 4, CO)
        z_out[d - 1] = jnp.concatenate([gk[there], gv[there]], axis=0).astype(BF16)
        start(z_out.at[d - 1], z_in.at[d - 1], RS_Z + d - 1, zs[d - 1])
    pass_back(5, 7)
    for d in (1, 2, 3):
        copy(z_out.at[d - 1], z_in.at[d - 1], RS_Z + d - 1, zs[d - 1]).wait_recv()
    here = piece(y, z, CO)
    arrived = z_in[0].astype(F32) + z_in[1].astype(F32) + z_in[2].astype(F32)
    coarse_row[0] = gk[here] + arrived[0:CO]
    coarse_row[1] = gv[here] + arrived[CO:]

    def fold(h, _):
        cols = head_cols(h)
        for side in range(2):
            number, hop, src, _, dst = back(side, h)
            copy(dst, dst, number, beside[side]).wait_recv()
            departed(side, number, hop, src)
            copy(
                back_out.at[side, h, 0], back_in.at[side, h, 0], BACK_K + side * HEADS + h,
                beside[side],
            ).wait()
        for n, (mine, target) in enumerate(((own_k, of_k), (own_v, of_v))):
            parts = [
                mine[h, side * WIN : (side + 1) * WIN] + back_in[side, h, n].astype(F32)
                for side in range(2)
            ]
            target[:, cols] = jnp.concatenate(
                parts + [coarse_row[n, :, cols]], axis=0
            ).astype(BF16)
        return 0

    every_head(fold, 0, 0, HEADS)
    for c in range(CHUNKS):
        for side in range(2):
            number, hop, src, _, _ = chunk(side, c)
            departed(side, number, hop, src)
    for c in pending:
        c.wait_send()


def deliver(a, b, c, d, to_a, to_b, to_c, to_d, held, arrive, leave):
    pairs = ((a, to_a), (b, to_b), (c, to_c), (d, to_d))
    inward = [pltpu.make_async_copy(p[0], held.at[n], arrive.at[n]) for n, p in enumerate(pairs)]
    outward = [pltpu.make_async_copy(held.at[n], p[1], leave.at[n]) for n, p in enumerate(pairs)]
    for c in inward:
        c.start()
    for n in range(4):
        inward[n].wait()
        outward[n].start()
    for c in outward:
        c.wait()


def on_device(query_rows, key_rows, value_rows, scale_index, norm_gain, cotangent):
    full = jax.ShapeDtypeStruct((FINE + CO, COLS), BF16)
    whole = pl.BlockSpec(memory_space=pltpu.VMEM)
    scratch = [
        pltpu.VMEM((RIM, COLS), BF16),
        pltpu.VMEM((RIM, COLS), BF16),
        pltpu.VMEM((64, 16, COLS), BF16),
        pltpu.VMEM((COARSE, COLS), BF16),
        pltpu.VMEM((COARSE, COLS), BF16),
        pltpu.VMEM((3, SPAN, BLOCK), F32),
        pltpu.VMEM((SLOTS, COARSE), F32),
        pltpu.VMEM((HEADS, HEAD_DIM, FINE), F32),
        pltpu.VMEM((HEADS, HEAD_DIM, FINE), BF16),
        pltpu.VMEM((HEADS, HEAD_DIM, FINE), BF16),
        pltpu.VMEM((HEADS, 1, FINE), F32),
        pltpu.VMEM((HEADS, 1, FINE), F32),
        pltpu.VMEM((HEADS, HEAD_DIM, FINE), F32),
        pltpu.VMEM((16, FINE), F32),
        pltpu.VMEM((3, 16, FINE), F32),
        pltpu.VMEM((2, CO, COLS), F32),
        pltpu.VMEM((SLOTS, COLS), BF16),
        pltpu.VMEM((SLOTS, COLS), BF16),
        pltpu.VMEM((COARSE, COLS), F32),
        pltpu.VMEM((COARSE, COLS), F32),
        pltpu.VMEM((HEADS, 1, FINE), F32),
        pltpu.VMEM((HEADS, 1, FINE), F32),
        pltpu.VMEM((HEADS, HEAD_DIM, FINE), F32),
        pltpu.VMEM((HEADS, FINE, HEAD_DIM), F32),
        pltpu.VMEM((HEADS, FINE, HEAD_DIM), F32),
        pltpu.VMEM((2, BLOCK, COLS), BF16),
        pltpu.VMEM((2, BLOCK, COLS), BF16),
        pltpu.VMEM((4, BLOCK, COLS), BF16),
        pltpu.VMEM((4, BLOCK, COLS), BF16),
        pltpu.VMEM((3, 2, 32, COLS), BF16),
        pltpu.VMEM((3, 2, 32, COLS), BF16),
        pltpu.VMEM((3, 2 * CO, COLS), BF16),
        pltpu.VMEM((3, 2 * CO, COLS), BF16),
        pltpu.VMEM((2, HEADS, 2, WIN, HEAD_DIM), BF16),
        pltpu.VMEM((2, HEADS, 2, WIN, HEAD_DIM), BF16),
        pltpu.VMEM((CHUNKS, CHUNK, COLS), BF16),
        pltpu.VMEM((HEADS, WIN, HEAD_DIM), BF16),
        pltpu.SemaphoreType.DMA((COPIES,)),
        pltpu.SemaphoreType.DMA((COPIES,)),
    ]
    results = pl.pallas_call(
        kernel,
        out_shape=[full] * 4,
        in_specs=[whole] * 6,
        out_specs=[whole] * 4,
        scratch_shapes=scratch,
        compiler_params=pltpu.CompilerParams(
            collective_id=0, has_side_effects=True, vmem_limit_bytes=56 * 1024 * 1024
        ),
    )(query_rows, key_rows, value_rows, cotangent, norm_gain, scale_index)
    anywhere = pl.BlockSpec(memory_space=pl.ANY)
    return tuple(pl.pallas_call(
        deliver,
        out_shape=[full] * 4,
        in_specs=[anywhere] * 4,
        out_specs=[anywhere] * 4,
        scratch_shapes=[
            pltpu.VMEM((4, FINE + CO, COLS), BF16),
            pltpu.SemaphoreType.DMA((4,)),
            pltpu.SemaphoreType.DMA((4,)),
        ],
    )(*results))


def solution(mesh):
    both = P("space", "scale")
    return jax.shard_map(
        on_device, mesh=mesh, in_specs=(both, both, both, P(), P("scale"), both),
        out_specs=(both, both, both, both), check_vma=False,
    )
```
